128 devices in a mesh: req: 32 (over x, z, core), head: 4 (over y).
Axes of the slice: x: 4, y: 4, z: 4, core: 2. Of those that a mesh axis runs over, the one named last changes fastest.
Arguments:
- prompt_query_latents: bfloat16 [16384, 1536], P(('req', 'head')), may hold values from -6 to 6
- prompt_latents: bfloat16 [16384, 512], P(('req', 'head')), may hold values from -320 to 320
- prompt_rotary_keys: bfloat16 [64, 16384], P(None, ('req', 'head')), may hold values from -6 to 6
- positions: int32 [16384], P(('req', 'head')), may hold values from 0 to 511, as said below
- query_up_weight: bfloat16 [1536, 12288], P(None, 'head'), may hold values from -0.15625 to 0.15625
- key_up_weight: bfloat16 [512, 8192], P(None, 'head'), may hold values from -0.25 to 0.25
- value_up_weight: bfloat16 [512, 8192], P(None, 'head'), may hold values from -0.25 to 0.25
- decode_queries: bfloat16 [2048, 12288], P('req', 'head'), may hold values from -6 to 6
- decode_owner_index: int32 [2048], P('req'), may hold values from 0 to 31, as said below
- decode_cache_slot: int32 [2048], P('req'), may hold values from 0 to 63, as said below
- latent_cache_rows: bfloat16 [2048, 256, 512], P('req'), may hold values from -320 to 320
- rotated_cache_keys: bfloat16 [2048, 64, 256], P('req'), may hold values from -6 to 6
- cache_live_lengths: int32 [2048], P('req'), may hold values from 1 to 256
Outputs:
- prompt_attention_output: bfloat16 [16384, 8192], P('req', 'head')
- decode_out: bfloat16 [2048, 8192], P('req', 'head')
The draws below stay inside these ranges and needn't reach their ends.
Inputs may be any that keep to these rules, and one draw needn't show every extreme that they name: `positions`: a position is 0 where a prompt begins, always at the first token of a block and, from the second block on, at other tokens too, and otherwise one more than the previous token's; the first block holds one whole prompt. `decode_owner_index`: each entry device's 64 requests name 16 owners, each exactly 4 times; every pair of owner and slot is named by exactly one request. `decode_cache_slot`: see decode_owner_index.
All inputs are finite; a program needn't handle non-finite values.
Results may differ from the reference program's by a relative error of at most 0.012.
The reference program's roundings to bfloat16 on the way count: a program that leaves them out, or rounds other values in their place, can miss the bound.
Values may be sent and summed in bfloat16 or wider, within the bound.
No kernel may reach another device: no remote copies, remote signals or barrier semaphores. Data moves between devices by JAX's collectives and lax.ppermute only.
A program may use at most 192 MiB of HBM per device.

```python
import jax
import jax.numpy as jnp
from jax import lax

H = 64
QUERY_LATENT = 1536
D_C = 512
D_NOPE = 128
D_ROPE = 64
D_V = 128
PROMPT_BLOCK = 512
PROMPT_TOKENS = 16384
DEC_DEV = 64
DEC_ROWS = 2048
MOST = 4
CMAX = 256
N_REQ = 32


def routing_tables(key):
    group_count = DEC_DEV // MOST
    key_one, key_two, key_three = jax.random.split(key, 3)
    owner_order = jax.random.permutation(key_one, N_REQ)
    offsets = jax.random.permutation(key_two, N_REQ)[:group_count]
    source = jnp.arange(N_REQ, dtype=jnp.int32)[:, None]
    column = jnp.arange(DEC_DEV, dtype=jnp.int32)[None, :]
    group_index = column // MOST
    owner_table = owner_order[(source + offsets[group_index]) % N_REQ]
    slot_table = jnp.broadcast_to(column, (N_REQ, DEC_DEV))
    shuffle = jax.random.permutation(key_three, slot_table, axis=1, independent=True)
    owner_table = jnp.take_along_axis(owner_table, shuffle, axis=1).reshape(-1)
    slot_table = jnp.take_along_axis(slot_table, shuffle, axis=1).reshape(-1)
    return (owner_table.astype(jnp.int32), slot_table.astype(jnp.int32))


def draw_decode_owner_index(key, part):
    return routing_tables(key)[0]


def draw_decode_cache_slot(key, part):
    return routing_tables(key)[1]


def draw_cache_live_lengths(key, part):
    key = jax.random.fold_in(key, 5)
    key_one, key_two, key_three = jax.random.split(key, 3)
    factor = jax.random.randint(key_one, (N_REQ, 1), 1, 5)
    raw_draw = jax.random.randint(key_two, (N_REQ, DEC_DEV), 0, CMAX)
    lengths = (1 + raw_draw * factor // 4).reshape(-1)
    chosen = jax.random.randint(key_three, (), 0, DEC_ROWS)
    lengths = jnp.where(jnp.arange(DEC_ROWS) == chosen, CMAX, lengths)
    return lengths.astype(jnp.int32)


def draw_positions(key, part):
    key = jax.random.fold_in(key, 7)
    token_index = jnp.arange(PROMPT_TOKENS, dtype=jnp.int32)
    starts = jax.random.randint(key, (PROMPT_TOKENS,), 0, max(PROMPT_BLOCK // 2, 2))
    begins = (starts == 0) & (token_index >= PROMPT_BLOCK) | (token_index % PROMPT_BLOCK == 0)
    last_begin = lax.cummax(jnp.where(begins, token_index, 0), axis=0)
    return (token_index - last_begin).astype(jnp.int32)


def latent_draw(key, shape):
    key_one = jax.random.fold_in(key, 0)
    base_draw = jax.random.normal(key_one, shape, jnp.float32)
    return jnp.clip(base_draw, -320.0, 320.0).astype(jnp.bfloat16)


def draw_latent_cache_rows(key, part):
    key = jax.random.fold_in(key, 11)
    return latent_draw(key, (DEC_ROWS, CMAX, D_C))


def draw_prompt_latents(key, part):
    key = jax.random.fold_in(key, 13)
    return latent_draw(key, (PROMPT_TOKENS, D_C))


def block_levels(stream_key, extent, cuts, low, top_value):
    level = 1.0
    for dim, shards_of in cuts:
        heights = jax.random.uniform(jax.random.fold_in(jax.random.fold_in(stream_key, 6), dim), (shards_of,), jnp.float32, low / len(cuts), top_value / len(cuts))
        level = level * jnp.repeat(jnp.exp(heights), extent[dim] // shards_of).reshape((-1,) + (1,) * (len(extent) - 1 - dim))
    return level


def scatter_about(rng, dims, scale, bound, shards=(), kind=jnp.bfloat16):
    gain = block_levels(rng, dims, shards, -0.22, 0.18) if shards else 1.0
    values = jax.random.normal(rng, dims, jnp.float32) * scale * gain
    return jnp.minimum(jnp.maximum(values, -bound), bound).astype(kind)


def setup_inputs(seed: int = 0) -> dict:
    keys = jax.random.split(jax.random.key(seed), 14)
    return {
        "prompt_query_latents": scatter_about(keys[0], (PROMPT_TOKENS, QUERY_LATENT), 1.0, 6.0, ((0, 128),)),
        "prompt_latents": draw_prompt_latents(jax.random.fold_in(keys[13], 71), 0),
        "prompt_rotary_keys": scatter_about(keys[2], (D_ROPE, PROMPT_TOKENS), 1.0, 6.0, ((1, 128),)),
        "positions": draw_positions(jax.random.fold_in(keys[13], 71), 0),
        "query_up_weight": scatter_about(keys[4], (QUERY_LATENT, H * (D_NOPE + D_ROPE)), QUERY_LATENT ** -0.5, 0.15625, ((1, 4),)),
        "key_up_weight": scatter_about(keys[5], (D_C, H * D_NOPE), D_C ** -0.5, 0.25, ((1, 4),)),
        "value_up_weight": scatter_about(keys[6], (D_C, H * D_V), D_C ** -0.5, 0.25, ((1, 4),)),
        "decode_queries": scatter_about(keys[7], (DEC_ROWS, H * (D_NOPE + D_ROPE)), 1.0, 6.0, ((0, 32), (1, 4))),
        "decode_owner_index": draw_decode_owner_index(jax.random.fold_in(keys[13], 71), 0),
        "decode_cache_slot": draw_decode_cache_slot(jax.random.fold_in(keys[13], 71), 0),
        "latent_cache_rows": draw_latent_cache_rows(jax.random.fold_in(keys[13], 71), 0),
        "rotated_cache_keys": scatter_about(keys[11], (DEC_ROWS, D_ROPE, CMAX), 1.0, 6.0, ((0, 32),)),
        "cache_live_lengths": draw_cache_live_lengths(jax.random.fold_in(keys[13], 71), 0),
    }


ROPE_BASE = 10000.0


def rotate(values, position):
    half_width = values.shape[-1] // 2
    frequency = ROPE_BASE ** (-jnp.arange(half_width, dtype=jnp.float32) / half_width)
    angles = position.astype(jnp.float32)[..., None] * frequency
    cosines = jnp.cos(angles)
    sine_term = jnp.sin(angles)
    first_half = values[..., :half_width]
    second_half = values[..., half_width:]
    return jnp.concatenate([first_half * cosines - second_half * sine_term, first_half * sine_term + second_half * cosines], axis=-1)


def rounded(values):
    return lax.optimization_barrier(values.astype(jnp.bfloat16)).astype(jnp.float32)


def reference(prompt_query_latents, prompt_latents, prompt_rotary_keys, positions, query_up_weight, key_up_weight, value_up_weight, decode_queries, decode_owner_index, decode_cache_slot, latent_cache_rows, rotated_cache_keys, cache_live_lengths):
    score_scale = (D_NOPE + D_ROPE) ** -0.5

    def prefill_block(pieces):
        query_rows, latent_rows, rope_cols, block_place = pieces
        queries = jnp.dot(query_rows, query_up_weight, preferred_element_type=jnp.float32).reshape(PROMPT_BLOCK, H, D_NOPE + D_ROPE)
        query_rope = rotate(queries[..., D_NOPE:], block_place[:, None])
        queries = rounded(jnp.concatenate([queries[..., :D_NOPE], query_rope], axis=-1))
        key_nope = rounded(jnp.dot(latent_rows, key_up_weight, preferred_element_type=jnp.float32)).reshape(PROMPT_BLOCK, H, D_NOPE)
        value_rows = rounded(jnp.dot(latent_rows, value_up_weight, preferred_element_type=jnp.float32)).reshape(PROMPT_BLOCK, H, D_V)
        key_rope = rounded(rotate(rope_cols.T.astype(jnp.float32), block_place))
        scores = (jnp.einsum('shd,thd->hst', queries[..., :D_NOPE], key_nope) + jnp.einsum('shd,td->hst', queries[..., D_NOPE:], key_rope)) * score_scale
        token_index = jnp.arange(PROMPT_BLOCK, dtype=jnp.int32)
        visible = (token_index[None, :] <= token_index[:, None]) & (token_index[None, :] >= token_index[:, None] - block_place[:, None])
        scores = jnp.where(visible[None], scores, -jnp.inf)
        weights = rounded(jax.nn.softmax(scores, axis=-1))
        return jnp.einsum('hst,thd->shd', weights, value_rows).astype(jnp.bfloat16).reshape(PROMPT_BLOCK, H * D_V)

    prompt_attention_output = lax.map(prefill_block, (
        prompt_query_latents.reshape(N_REQ, PROMPT_BLOCK, QUERY_LATENT),
        prompt_latents.reshape(N_REQ, PROMPT_BLOCK, D_C),
        prompt_rotary_keys.reshape(D_ROPE, N_REQ, PROMPT_BLOCK).transpose(1, 0, 2),
        positions.reshape(N_REQ, PROMPT_BLOCK))).reshape(PROMPT_TOKENS, H * D_V)

    key_map = key_up_weight.astype(jnp.float32).reshape(D_C, H, D_NOPE)
    value_map = value_up_weight.astype(jnp.float32).reshape(D_C, H, D_V)
    cache_index = (decode_owner_index * DEC_DEV + decode_cache_slot).astype(jnp.int32)

    def decode_row(pieces):
        query_row, cache_row = pieces
        query_heads = query_row.astype(jnp.float32).reshape(H, D_NOPE + D_ROPE)
        latent_query = rounded(jnp.einsum('hd,chd->hc', query_heads[:, :D_NOPE], key_map))
        latent = lax.dynamic_index_in_dim(latent_cache_rows, cache_row, 0, keepdims=False).astype(jnp.float32)
        rope_rows = lax.dynamic_index_in_dim(rotated_cache_keys, cache_row, 0, keepdims=False).astype(jnp.float32)
        length = lax.dynamic_index_in_dim(cache_live_lengths, cache_row, 0, keepdims=False)
        scores = (jnp.einsum('hc,tc->ht', latent_query, latent) + jnp.einsum('hd,dt->ht', query_heads[:, D_NOPE:], rope_rows)) * score_scale
        visible = jnp.arange(CMAX, dtype=jnp.int32) < length
        scores = jnp.where(visible[None, :], scores, -jnp.inf)
        weights = rounded(jax.nn.softmax(scores, axis=-1))
        latent_out = rounded(jnp.einsum('ht,tc->hc', weights, latent))
        return jnp.einsum('hc,chd->hd', latent_out, value_map).astype(jnp.bfloat16).reshape(H * D_V)

    decode_out = lax.map(decode_row, (decode_queries, cache_index))
    return prompt_attention_output, decode_out
```

```python
import functools
import math

import jax
import jax.numpy as jnp
import numpy as np
from jax import lax
from jax.experimental import pallas as pl
from jax.experimental.pallas import tpu as pltpu
from jax.sharding import PartitionSpec as P

D_C = 512
D_NOPE = 128
D_ROPE = 64
D_V = 128
D_Q = 1536
HEADS = 16
TOKENS = 512
CHUNK = 128
ROWS = 64
MOST = 4
SLOTS = 64
CMAX = 256
PEERS = 32
PACK = D_Q + D_C + 128
SEND = 1536 + 128
RET = 1024
ROPE_BASE = 10000.0
SCALE = (D_NOPE + D_ROPE) ** -0.5
SCALE_LOG2 = SCALE * math.log2(math.e)
MASKED = -1e30
F32 = jnp.float32
BF16 = jnp.bfloat16
MIB = 1024 * 1024


def iota(shape, dim):
    return lax.broadcasted_iota(jnp.int32, shape, dim)


def dot(a, b, dims=((1,), (0,))):
    return lax.dot_general(a, b, (dims, ((), ())), preferred_element_type=F32)


def column_of(row):
    n = row.shape[1]
    eye = iota((n, n), 0) == iota((n, n), 1)
    return jnp.sum(jnp.where(eye, row, 0), axis=1, keepdims=True)


def pack_kernel(x_ref, l_ref, rk_ref, pos_ref, freq_ref, q_ref, owner_ref, slot_ref, packed_ref, send_ref):
    packed_ref[:, :D_Q] = x_ref[...]
    packed_ref[:, D_Q:D_Q + D_C] = l_ref[...]
    pos = pos_ref[...]
    angle = pos.astype(F32) * freq_ref[...]
    cos, sin = jnp.cos(angle), jnp.sin(angle)
    keys = rk_ref[...].astype(F32)
    first, second = keys[:32], keys[32:]
    high = (pos >> 4).astype(F32)
    low = (pos & 15).astype(F32)
    place = iota((64, CHUNK), 0)
    tail = jnp.where(place == 0, high, jnp.where(place == 1, low, 0.0))
    block = jnp.concatenate([first * cos - second * sin, first * sin + second * cos, tail], axis=0)
    packed_ref[:, D_Q + D_C:] = block.T.astype(BF16)

    owner = owner_ref[...]
    owner_col = column_of(owner)
    same = owner_col == owner
    before = iota((ROWS, ROWS), 0) < iota((ROWS, ROWS), 1)
    rank = jnp.sum(jnp.where(same & before, 1, 0), axis=0, keepdims=True)
    target = owner * (2 * MOST) + rank
    target = jnp.concatenate([target, target + MOST], axis=1)
    placing = iota((PEERS * 2 * MOST, 2 * ROWS), 0) == target
    queries = jnp.concatenate([q_ref[:, :1536], q_ref[:, 1536:]], axis=0)
    send_ref[:, :1536] = dot(placing.astype(BF16), queries).astype(BF16)
    slot = slot_ref[...] + 1
    slot = jnp.concatenate([slot, slot], axis=1)
    slot_col = jnp.sum(jnp.where(placing, slot, 0), axis=1, keepdims=True)
    send_ref[:, 1536:] = jnp.broadcast_to(slot_col.astype(F32), (PEERS * 2 * MOST, 128)).astype(BF16)


def split_pair(three):
    low_lane = iota((three.shape[0], 128), 1) < 64
    second, third = three[:, 128:256], three[:, 256:]
    rotary = jnp.where(low_lane, second, third)
    odd = pltpu.roll(jnp.where(low_lane, third, second), 64, 1)
    return three[:, :128], odd, rotary


SLOTS_PER_STEP = 8


def decode_kernel(recv_ref, kup_ref, vup_ref, lat_ref, rk_ref, len_ref, out_ref, lq_ref, qr_ref, lo_ref):
    step = pl.program_id(0)
    rows = PEERS * 2 * MOST

    def slot_onehot():
        slot_col = recv_ref[:, 1536:].astype(jnp.int32)
        lane = iota((rows, 128), 1)
        hit = slot_col == lane + 1
        half = (iota((rows, 128), 0) & 7) < MOST
        return hit & half, hit & jnp.logical_not(half)

    @pl.when(step == 0)
    def _():
        first, second = slot_onehot()
        for side, hit in enumerate((first, second)):
            spread = jnp.where(hit, 1.0, 0.0).T[:SLOTS].astype(BF16)
            queries = dot(spread, recv_ref[:, :1536])
            for pair in range(4):
                even, odd, rotary = split_pair(queries[:, pair * 384:(pair + 1) * 384])
                for sub, nope in enumerate((even, odd)):
                    head = side * 8 + pair * 2 + sub
                    latent = dot(nope.astype(BF16), kup_ref[:, head * 128:(head + 1) * 128], ((1,), (1,)))
                    latent = latent.astype(BF16).astype(F32)
                    for part in range(4):
                        lq_ref[part, head * SLOTS:(head + 1) * SLOTS, :] = latent[:, part * 128:(part + 1) * 128]
                    qr_ref[head * SLOTS:(head + 1) * SLOTS, :] = rotary if sub == 0 else pltpu.roll(rotary, 64, 1)

    scores = []
    for i in range(SLOTS_PER_STEP):
        slot = step * SLOTS_PER_STEP + i
        latent = jnp.concatenate(
            [lq_ref[part, pl.ds(slot, HEADS, stride=SLOTS), :].astype(BF16) for part in range(4)], axis=1)
        rotary = qr_ref[pl.ds(slot, HEADS, stride=SLOTS), :].astype(BF16)
        score = dot(latent, lat_ref[i], ((1,), (1,))) + dot(rotary[:, :D_ROPE], rk_ref[i])
        score = jnp.where(iota((HEADS, CMAX), 1) < len_ref[slot], score * SCALE, MASKED)
        scores.append(score)
    weights = []
    for i in range(SLOTS_PER_STEP):
        score = scores[i]
        raised = jnp.exp(score - jnp.max(score, axis=1, keepdims=True))
        weights.append((raised / jnp.sum(raised, axis=1, keepdims=True)).astype(BF16))
    for i in range(SLOTS_PER_STEP):
        slot = step * SLOTS_PER_STEP + i
        latent_out = dot(weights[i], lat_ref[i])
        latent_out = latent_out.astype(BF16).astype(F32)
        for part in range(4):
            lo_ref[part, pl.ds(slot, HEADS, stride=SLOTS), :] = latent_out[:, part * 128:(part + 1) * 128]

    @pl.when(step == pl.num_programs(0) - 1)
    def _():
        outs = []
        for head in range(HEADS):
            latent_out = jnp.concatenate(
                [lo_ref[part, head * SLOTS:(head + 1) * SLOTS, :].astype(BF16) for part in range(4)], axis=1)
            outs.append(dot(latent_out, vup_ref[:, head * 128:(head + 1) * 128]).astype(BF16))
        outs = jnp.concatenate([jnp.concatenate(outs[:8], axis=1), jnp.concatenate(outs[8:], axis=1)], axis=0)
        first, second = slot_onehot()
        spread = jnp.concatenate([jnp.where(first, 1.0, 0.0)[:, :SLOTS], jnp.where(second, 1.0, 0.0)[:, :SLOTS]], axis=1)
        out_ref[...] = dot(spread.astype(BF16), outs).astype(BF16)


def unplace_kernel(ret_ref, owner_ref, out_ref):
    owner = owner_ref[...]
    owner_col = column_of(owner)
    before = iota((ROWS, ROWS), 1) < iota((ROWS, ROWS), 0)
    rank = jnp.sum(jnp.where((owner_col == owner) & before, 1, 0), axis=1, keepdims=True)
    target = owner_col * (2 * MOST) + rank
    lane = iota((ROWS, PEERS * 2 * MOST), 1)
    for side in range(2):
        spread = jnp.where(lane == target + side * MOST, 1.0, 0.0).astype(BF16)
        out_ref[:, side * RET:(side + 1) * RET] = dot(spread, ret_ref[...]).astype(BF16)


GROUP = 4


def project_kernel(head_ref, own_ref, left_ref, right_ref, top_ref, bottom_ref, freq_ref, wq_ref, wk_ref, wv_ref,
                   qn_ref, qr_ref, k_ref, v_ref, kr_ref, x_ref, cos_ref, sin_ref):
    @pl.when(pl.program_id(0) == 0)
    def _():
        me = head_ref[0]
        x_ref[me] = own_ref[...]
        x_ref[(me + 3) & 3] = left_ref[...]
        x_ref[(me + 1) & 3] = right_ref[...]
        x_ref[(me + 2) & 3, :64] = top_ref[...]
        x_ref[(me + 2) & 3, 64:] = bottom_ref[...]
        extra = x_ref[:, :, D_Q + D_C:].reshape(TOKENS, 128)
        kr_ref[...] = extra
        turned = extra.astype(F32).T
        pos = turned[64:65] * 16.0 + turned[65:66]
        angle = pos * freq_ref[...]
        cos, sin = jnp.cos(angle), jnp.sin(angle)
        cos_ref[...] = jnp.concatenate([cos, cos, cos, cos], axis=0).T
        sin_ref[...] = jnp.concatenate([-sin, sin, -sin, sin], axis=0).T

    half = TOKENS // 2
    lane = iota((half, 128), 1) & 63
    for part in range(2):
        rows = slice(part * half, (part + 1) * half)
        x = x_ref[2 * part:2 * part + 2, :, :].reshape(half, PACK)
        queries = dot(x[:, :D_Q], wq_ref[...])
        cos, sin = cos_ref[rows, :], sin_ref[rows, :]
        for pair in range(GROUP // 2):
            even, odd, rotary = split_pair(queries[:, pair * 384:(pair + 1) * 384])
            qn_ref[rows, pair * 256:pair * 256 + 128] = even.astype(BF16)
            qn_ref[rows, pair * 256 + 128:pair * 256 + 256] = odd.astype(BF16)
            swapped = jnp.where(lane < 32, pltpu.roll(rotary, 96, 1), pltpu.roll(rotary, 32, 1))
            qr_ref[rows, pair * 128:(pair + 1) * 128] = (rotary * cos + swapped * sin).astype(BF16)
        latents = x[:, D_Q:D_Q + D_C]
        k_ref[rows, :] = dot(latents, wk_ref[...]).astype(BF16)
        v_ref[rows, :] = dot(latents, wv_ref[...]).astype(BF16)


def attention_kernel(qn_ref, qr_ref, k_ref, v_ref, kr_ref, out_ref, bias_ref, key_ref, value_ref):
    half = TOKENS // 2

    @pl.when(pl.program_id(0) == 0)
    def _():
        extra = kr_ref[...].astype(F32)
        pos = (extra[:, 64:65] * 16.0 + extra[:, 65:66]).astype(jnp.int32)
        query, key = iota((TOKENS, TOKENS), 0), iota((TOKENS, TOKENS), 1)
        bias_ref[...] = jnp.where((key <= query) & (key >= query - pos), 0.0, MASKED)
        low_lane = iota((TOKENS, 128), 1) < 64
        keep = jnp.where(low_lane, extra, 0.0)
        key_ref[0, :, 128:] = keep.astype(BF16)
        key_ref[1, :, 128:] = pltpu.roll(keep, 64, 1).astype(BF16)
        value_ref[:, :, 128:] = jnp.ones((2, TOKENS, 128), BF16)

    for sub in range(2):
        lanes = slice(sub * 128, (sub + 1) * 128)
        key_ref[sub, :, :128] = k_ref[:, lanes]
        value_ref[sub, :, :128] = v_ref[:, lanes]
    for sub in range(2):
        lanes = slice(sub * 128, (sub + 1) * 128)
        for part in range(2):
            rows = slice(part * half, (part + 1) * half)
            seen = (part + 1) * half
            query = jnp.concatenate([qn_ref[rows, lanes], qr_ref[rows, :]], axis=1)
            score = dot(query, key_ref[sub, :seen, :], ((1,), (1,))) + bias_ref[rows, :seen]
            top = jnp.max(score, axis=1, keepdims=True)
            raised = jnp.exp2((score - top) * SCALE_LOG2).astype(BF16)
            total = dot(raised, value_ref[sub, :seen, :])
            out_ref[rows, lanes] = (total[:, :128] / total[:, 128:]).astype(BF16)


def whole(shape):
    return pl.BlockSpec(shape, lambda *_: (0,) * len(shape))


def params(mib):
    return pltpu.CompilerParams(vmem_limit_bytes=mib * MIB)


def smem():
    return pl.BlockSpec(memory_space=pltpu.SMEM)


def on_device(x, latents, rotary_keys, positions, wq, wk, wv, queries, owner, slot, cache, cache_rope, lengths):
    me = lax.axis_index("head").astype(jnp.int32).reshape(1)
    freq = jnp.asarray(ROPE_BASE ** (-np.arange(32) / 32.0), F32).reshape(32, 1)
    owner_row, slot_row = owner.reshape(1, ROWS), slot.reshape(1, ROWS)
    packed, send = pl.pallas_call(
        pack_kernel,
        out_shape=(
            jax.ShapeDtypeStruct((CHUNK, PACK), BF16),
            jax.ShapeDtypeStruct((PEERS * 2 * MOST, SEND), BF16),
        ),
        compiler_params=params(24),
        name="pack",
    )(x, latents, rotary_keys, positions.reshape(1, CHUNK), freq, queries, owner_row, slot_row)

    up = [(i, (i + 1) % 4) for i in range(4)]
    down = [(i, (i + 3) % 4) for i in range(4)]
    left = lax.ppermute(packed, "head", up)
    right = lax.ppermute(packed, "head", down)
    recv = lax.all_to_all(send, "req", 0, 0, tiled=True)
    top = lax.ppermute(left[:64], "head", up)
    bottom = lax.ppermute(right[64:], "head", down)

    returned = pl.pallas_call(
        decode_kernel,
        grid=(SLOTS // SLOTS_PER_STEP,),
        in_specs=[
            whole((PEERS * 2 * MOST, SEND)),
            whole((D_C, HEADS * D_NOPE)),
            whole((D_C, HEADS * D_V)),
            pl.BlockSpec((SLOTS_PER_STEP, CMAX, D_C), lambda i: (i, 0, 0)),
            pl.BlockSpec((SLOTS_PER_STEP, D_ROPE, CMAX), lambda i: (i, 0, 0)),
            smem(),
        ],
        out_specs=whole((PEERS * 2 * MOST, RET)),
        out_shape=jax.ShapeDtypeStruct((PEERS * 2 * MOST, RET), BF16),
        scratch_shapes=[
            pltpu.VMEM((4, HEADS * SLOTS, 128), F32),
            pltpu.VMEM((HEADS * SLOTS, 128), F32),
            pltpu.VMEM((4, HEADS * SLOTS, 128), F32),
        ],
        compiler_params=params(40),
        name="decode",
    )(recv, wk, wv, cache, cache_rope, lengths)
    returned = lax.all_to_all(returned, "req", 0, 0, tiled=True)

    steps = HEADS // GROUP
    qn, qr, keys, values, key_rope = pl.pallas_call(
        project_kernel,
        grid=(steps,),
        in_specs=[
            smem(),
            whole((CHUNK, PACK)),
            whole((CHUNK, PACK)),
            whole((CHUNK, PACK)),
            whole((64, PACK)),
            whole((64, PACK)),
            whole((32, 1)),
            pl.BlockSpec((D_Q, GROUP * 192), lambda i: (0, i)),
            pl.BlockSpec((D_C, GROUP * 128), lambda i: (0, i)),
            pl.BlockSpec((D_C, GROUP * 128), lambda i: (0, i)),
        ],
        out_specs=(
            pl.BlockSpec((TOKENS, GROUP * 128), lambda i: (0, i)),
            pl.BlockSpec((TOKENS, GROUP * 64), lambda i: (0, i)),
            pl.BlockSpec((TOKENS, GROUP * 128), lambda i: (0, i)),
            pl.BlockSpec((TOKENS, GROUP * 128), lambda i: (0, i)),
            whole((TOKENS, 128)),
        ),
        out_shape=(
            jax.ShapeDtypeStruct((TOKENS, HEADS * 128), BF16),
            jax.ShapeDtypeStruct((TOKENS, HEADS * 64), BF16),
            jax.ShapeDtypeStruct((TOKENS, HEADS * 128), BF16),
            jax.ShapeDtypeStruct((TOKENS, HEADS * 128), BF16),
            jax.ShapeDtypeStruct((TOKENS, 128), BF16),
        ),
        scratch_shapes=[
            pltpu.VMEM((4, CHUNK, PACK), BF16),
            pltpu.VMEM((TOKENS, 128), F32),
            pltpu.VMEM((TOKENS, 128), F32),
        ],
        compiler_params=params(40),
        name="project",
    )(me, packed, left, right, top, bottom, freq, wq, wk, wv)

    prompt_out = pl.pallas_call(
        attention_kernel,
        grid=(HEADS // 2,),
        in_specs=[
            pl.BlockSpec((TOKENS, 256), lambda i: (0, i)),
            pl.BlockSpec((TOKENS, 128), lambda i: (0, i)),
            pl.BlockSpec((TOKENS, 256), lambda i: (0, i)),
            pl.BlockSpec((TOKENS, 256), lambda i: (0, i)),
            whole((TOKENS, 128)),
        ],
        out_specs=pl.BlockSpec((TOKENS, 256), lambda i: (0, i)),
        out_shape=jax.ShapeDtypeStruct((TOKENS, HEADS * D_V), BF16),
        scratch_shapes=[
            pltpu.VMEM((TOKENS, TOKENS), F32),
            pltpu.VMEM((2, TOKENS, 256), BF16),
            pltpu.VMEM((2, TOKENS, 256), BF16),
        ],
        compiler_params=params(32),
        name="attention",
    )(qn, qr, keys, values, key_rope)

    decode_out = pl.pallas_call(
        unplace_kernel,
        out_shape=jax.ShapeDtypeStruct((ROWS, HEADS * D_V), BF16),
        compiler_params=params(16),
        name="unplace",
    )(returned, owner_row)
    return prompt_out, decode_out


def solution(mesh):
    placed = (
        P(("req", "head"), None),
        P(("req", "head"), None),
        P(None, ("req", "head")),
        P(("req", "head")),
        P(None, "head"),
        P(None, "head"),
        P(None, "head"),
        P("req", "head"),
        P("req"),
        P("req"),
        P("req", None, None),
        P("req", None, None),
        P("req"),
    )
    return jax.shard_map(
        on_device,
        mesh=mesh,
        in_specs=placed,
        out_specs=(P("req", "head"), P("req", "head")),
        check_vma=False,
    )
```

```python
import math

import jax
import jax.numpy as jnp
import numpy as np
from jax import lax
from jax.experimental import pallas as pl
from jax.experimental.pallas import tpu as pltpu
from jax.sharding import PartitionSpec as P

D_C = 512
D_NOPE = 128
D_ROPE = 64
D_V = 128
D_Q = 1536
HEADS = 16
TOKENS = 512
CHUNK = 128
ROWS = 64
MOST = 4
SLOTS = 64
CMAX = 256
PEERS = 32
PACK = D_Q + D_C + 128
SEND = 1536 + 128
RET = 1024
ROPE_BASE = 10000.0
SCALE = (D_NOPE + D_ROPE) ** -0.5
SCALE_LOG2 = SCALE * math.log2(math.e)
MASKED = -1e30
F32 = jnp.float32
BF16 = jnp.bfloat16
MIB = 1024 * 1024


def iota(shape, dim):
    return lax.broadcasted_iota(jnp.int32, shape, dim)


def dot(a, b, dims=((1,), (0,))):
    return lax.dot_general(a, b, (dims, ((), ())), preferred_element_type=F32)


def column_of(row):
    n = row.shape[1]
    eye = iota((n, n), 0) == iota((n, n), 1)
    return jnp.sum(jnp.where(eye, row, 0), axis=1, keepdims=True)


def pack_kernel(x_ref, l_ref, rk_ref, pos_ref, freq_ref, after_ref, packed_ref):
    packed_ref[:, :D_Q] = x_ref[...]
    packed_ref[:, D_Q:D_Q + D_C] = l_ref[...]
    pos = pos_ref[...]
    angle = pos.astype(F32) * freq_ref[...]
    cos, sin = jnp.cos(angle), jnp.sin(angle)
    keys = rk_ref[...].astype(F32)
    first, second = keys[:32], keys[32:]
    high = (pos >> 4).astype(F32)
    low = (pos & 15).astype(F32)
    place = iota((64, CHUNK), 0)
    tail = jnp.where(place == 0, high, jnp.where(place == 1, low, 0.0))
    block = jnp.concatenate([first * cos - second * sin, first * sin + second * cos, tail], axis=0)
    packed_ref[:, D_Q + D_C:] = block.T.astype(BF16)


def place_kernel(q_ref, owner_ref, slot_ref, send_ref):
    owner = owner_ref[...]
    owner_col = column_of(owner)
    same = owner_col == owner
    before = iota((ROWS, ROWS), 0) < iota((ROWS, ROWS), 1)
    rank = jnp.sum(jnp.where(same & before, 1, 0), axis=0, keepdims=True)
    target = owner * (2 * MOST) + rank
    target = jnp.concatenate([target, target + MOST], axis=1)
    placing = iota((PEERS * 2 * MOST, 2 * ROWS), 0) == target
    queries = jnp.concatenate([q_ref[:, :1536], q_ref[:, 1536:]], axis=0)
    send_ref[:, :1536] = dot(placing.astype(BF16), queries).astype(BF16)
    slot = slot_ref[...] + 1
    slot = jnp.concatenate([slot, slot], axis=1)
    slot_col = jnp.sum(jnp.where(placing, slot, 0), axis=1, keepdims=True)
    send_ref[:, 1536:] = jnp.broadcast_to(slot_col.astype(F32), (PEERS * 2 * MOST, 128)).astype(BF16)


def split_pair(three):
    low_lane = iota((three.shape[0], 128), 1) < 64
    second, third = three[:, 128:256], three[:, 256:]
    rotary = jnp.where(low_lane, second, third)
    odd = pltpu.roll(jnp.where(low_lane, third, second), 64, 1)
    return three[:, :128], odd, rotary


SLOTS_PER_STEP = 8


def decode_kernel(recv_ref, kup_ref, vup_ref, lat_ref, rk_ref, len_ref, after_ref, out_ref, lq_ref, qr_ref, lo_ref):
    step = pl.program_id(0)
    rows = PEERS * 2 * MOST

    def slot_onehot():
        slot_col = recv_ref[:, 1536:].astype(jnp.int32)
        lane = iota((rows, 128), 1)
        hit = slot_col == lane + 1
        half = (iota((rows, 128), 0) & 7) < MOST
        return hit & half, hit & jnp.logical_not(half)

    @pl.when(step == 0)
    def _():
        first, second = slot_onehot()
        for side, hit in enumerate((first, second)):
            spread = jnp.where(hit, 1.0, 0.0).T[:SLOTS].astype(BF16)
            queries = dot(spread, recv_ref[:, :1536])
            for pair in range(4):
                even, odd, rotary = split_pair(queries[:, pair * 384:(pair + 1) * 384])
                for sub, nope in enumerate((even, odd)):
                    head = side * 8 + pair * 2 + sub
                    latent = dot(nope.astype(BF16), kup_ref[:, head * 128:(head + 1) * 128], ((1,), (1,)))
                    latent = latent.astype(BF16).astype(F32)
                    for part in range(4):
                        lq_ref[part, head * SLOTS:(head + 1) * SLOTS, :] = latent[:, part * 128:(part + 1) * 128]
                    qr_ref[head * SLOTS:(head + 1) * SLOTS, :] = rotary if sub == 0 else pltpu.roll(rotary, 64, 1)

    scores = []
    for i in range(SLOTS_PER_STEP):
        slot = step * SLOTS_PER_STEP + i
        latent = jnp.concatenate(
            [lq_ref[part, pl.ds(slot, HEADS, stride=SLOTS), :].astype(BF16) for part in range(4)], axis=1)
        rotary = qr_ref[pl.ds(slot, HEADS, stride=SLOTS), :].astype(BF16)
        score = dot(latent, lat_ref[i], ((1,), (1,))) + dot(rotary[:, :D_ROPE], rk_ref[i])
        score = jnp.where(iota((HEADS, CMAX), 1) < len_ref[slot], score * SCALE, MASKED)
        scores.append(score)
    weights = []
    for i in range(SLOTS_PER_STEP):
        score = scores[i]
        raised = jnp.exp(score - jnp.max(score, axis=1, keepdims=True))
        weights.append((raised / jnp.sum(raised, axis=1, keepdims=True)).astype(BF16))
    for i in range(SLOTS_PER_STEP):
        slot = step * SLOTS_PER_STEP + i
        latent_out = dot(weights[i], lat_ref[i])
        latent_out = latent_out.astype(BF16).astype(F32)
        for part in range(4):
            lo_ref[part, pl.ds(slot, HEADS, stride=SLOTS), :] = latent_out[:, part * 128:(part + 1) * 128]

    @pl.when(step == pl.num_programs(0) - 1)
    def _():
        outs = []
        for head in range(HEADS):
            latent_out = jnp.concatenate(
                [lo_ref[part, head * SLOTS:(head + 1) * SLOTS, :].astype(BF16) for part in range(4)], axis=1)
            outs.append(dot(latent_out, vup_ref[:, head * 128:(head + 1) * 128]).astype(BF16))
        outs = jnp.concatenate([jnp.concatenate(outs[:8], axis=1), jnp.concatenate(outs[8:], axis=1)], axis=0)
        first, second = slot_onehot()
        spread = jnp.concatenate([jnp.where(first, 1.0, 0.0)[:, :SLOTS], jnp.where(second, 1.0, 0.0)[:, :SLOTS]], axis=1)
        out_ref[...] = dot(spread.astype(BF16), outs).astype(BF16)


def unplace_kernel(ret_ref, owner_ref, out_ref):
    owner = owner_ref[...]
    owner_col = column_of(owner)
    before = iota((ROWS, ROWS), 1) < iota((ROWS, ROWS), 0)
    rank = jnp.sum(jnp.where((owner_col == owner) & before, 1, 0), axis=1, keepdims=True)
    target = owner_col * (2 * MOST) + rank
    lane = iota((ROWS, PEERS * 2 * MOST), 1)
    for side in range(2):
        spread = jnp.where(lane == target + side * MOST, 1.0, 0.0).astype(BF16)
        out_ref[:, side * RET:(side + 1) * RET] = dot(spread, ret_ref[...]).astype(BF16)


GROUP = 4


def project_kernel(count, chunks, freq_ref, wq_ref, wk_ref, wv_ref, qn_ref, qr_ref, k_ref, v_ref, kr_ref,
                   x_ref, cos_ref, sin_ref):
    rows = count * CHUNK

    @pl.when(pl.program_id(0) == 0)
    def _():
        for i, chunk in enumerate(chunks):
            x_ref[i * CHUNK:(i + 1) * CHUNK, :] = chunk[...]
        extra = x_ref[:, D_Q + D_C:]
        kr_ref[...] = extra.reshape(count, CHUNK, 128)
        turned = extra.astype(F32).T
        pos = turned[64:65] * 16.0 + turned[65:66]
        angle = pos * freq_ref[...]
        cos, sin = jnp.cos(angle), jnp.sin(angle)
        cos_ref[...] = jnp.concatenate([cos, cos, cos, cos], axis=0).T
        sin_ref[...] = jnp.concatenate([-sin, sin, -sin, sin], axis=0).T

    lane = iota((rows, 128), 1) & 63
    shape = (count, CHUNK, 128)
    queries = dot(x_ref[:, :D_Q], wq_ref[...])
    for pair in range(GROUP // 2):
        even, odd, rotary = split_pair(queries[:, pair * 384:(pair + 1) * 384])
        qn_ref[:, :, pair * 256:pair * 256 + 128] = even.astype(BF16).reshape(shape)
        qn_ref[:, :, pair * 256 + 128:pair * 256 + 256] = odd.astype(BF16).reshape(shape)
        swapped = jnp.where(lane < 32, pltpu.roll(rotary, 96, 1), pltpu.roll(rotary, 32, 1))
        turned = (rotary * cos_ref[...] + swapped * sin_ref[...]).astype(BF16)
        qr_ref[:, :, pair * 128:(pair + 1) * 128] = turned.reshape(shape)
    latents = x_ref[:, D_Q:D_Q + D_C]
    k_ref[...] = dot(latents, wk_ref[...]).astype(BF16).reshape(count, CHUNK, GROUP * 128)
    v_ref[...] = dot(latents, wv_ref[...]).astype(BF16).reshape(count, CHUNK, GROUP * 128)


def project_own_kernel(own_ref, freq_ref, wq_ref, wk_ref, wv_ref, *rest):
    project_kernel(1, (own_ref,), freq_ref, wq_ref, wk_ref, wv_ref, *rest)


def project_rest_kernel(right_ref, far_ref, left_ref, freq_ref, wq_ref, wk_ref, wv_ref, a, b, c, d, e, after, *rest):
    project_kernel(3, (right_ref, far_ref, left_ref), freq_ref, wq_ref, wk_ref, wv_ref, *rest)


TILE = 256


def attention_kernel(head_ref, qn_ref, qr_ref, k_ref, v_ref, kr_ref, out_ref, bias_ref, pair_ref):
    me = head_ref[0]
    place = [(c - me + 3) & 3 for c in range(4)]
    per_tile = TILE // CHUNK

    @pl.when(pl.program_id(0) == 0)
    def _():
        low_lane = iota((CHUNK, 128), 1) < 64
        for c in range(4):
            extra = kr_ref[place[c]].astype(F32)
            pos = (extra[:, 64:65] * 16.0 + extra[:, 65:66]).astype(jnp.int32)
            query, key = iota((CHUNK, TOKENS), 0) + c * CHUNK, iota((CHUNK, TOKENS), 1)
            bias_ref[c * CHUNK:(c + 1) * CHUNK, :] = jnp.where((key <= query) & (key >= query - pos), 0.0, MASKED)
            keep = jnp.where(low_lane, extra, 0.0)
            pair_ref[0, c] = keep.astype(BF16)
            pair_ref[1, c] = pltpu.roll(keep, 64, 1).astype(BF16)

    ones = jnp.ones((CHUNK, 128), BF16)
    for tile in range(TOKENS // TILE):
        for sub in range(2):
            lanes = slice(sub * 128, (sub + 1) * 128)
            mine = range(tile * per_tile, (tile + 1) * per_tile)
            seen = range((tile + 1) * per_tile)
            query = jnp.concatenate(
                [jnp.concatenate([qn_ref[place[c], :, lanes], qr_ref[place[c]]], axis=1) for c in mine], axis=0)
            keys = jnp.concatenate(
                [jnp.concatenate([k_ref[place[c], :, lanes], pair_ref[sub, c]], axis=1) for c in seen], axis=0)
            values = jnp.concatenate(
                [jnp.concatenate([v_ref[place[c], :, lanes], ones], axis=1) for c in seen], axis=0)
            rows = slice(tile * TILE, (tile + 1) * TILE)
            score = dot(query, keys, ((1,), (1,))) + bias_ref[rows, :len(seen) * CHUNK]
            top = jnp.max(score, axis=1, keepdims=True)
            raised = jnp.exp2((score - top) * SCALE_LOG2).astype(BF16)
            total = dot(raised, values)
            out_ref[rows, lanes] = (total[:, :128] / total[:, 128:]).astype(BF16)


def whole(shape):
    return pl.BlockSpec(shape, lambda *_: (0,) * len(shape))


def params(mib):
    return pltpu.CompilerParams(vmem_limit_bytes=mib * MIB)


def smem():
    return pl.BlockSpec(memory_space=pltpu.SMEM)


def anywhere():
    return pl.BlockSpec(memory_space=pl.ANY)


def project(count, kernel, chunks, freq, wq, wk, wv, into, after):
    first = 0 if into else 3
    shapes = [(HEADS * 128, GROUP * 128), (HEADS * 64, GROUP * 64), (HEADS * 128, GROUP * 128), (HEADS * 128, GROUP * 128)]
    inputs = list(chunks) + [freq, wq, wk, wv] + list(into) + list(after)
    n = len(chunks) + 4
    return pl.pallas_call(
        kernel,
        grid=(HEADS // GROUP,),
        in_specs=[whole((CHUNK, PACK))] * len(chunks) + [
            whole((32, 1)),
            pl.BlockSpec((D_Q, GROUP * 192), lambda i: (0, i)),
            pl.BlockSpec((D_C, GROUP * 128), lambda i: (0, i)),
            pl.BlockSpec((D_C, GROUP * 128), lambda i: (0, i)),
        ] + [anywhere()] * (len(into) + len(after)),
        out_specs=[pl.BlockSpec((count, CHUNK, block), lambda i: (first, 0, i)) for _, block in shapes]
        + [pl.BlockSpec((count, CHUNK, 128), lambda i: (first, 0, 0))],
        out_shape=[jax.ShapeDtypeStruct((4, CHUNK, width), BF16) for width, _ in shapes]
        + [jax.ShapeDtypeStruct((4, CHUNK, 128), BF16)],
        input_output_aliases={n + i: i for i in range(len(into))},
        scratch_shapes=[
            pltpu.VMEM((count * CHUNK, PACK), BF16),
            pltpu.VMEM((count * CHUNK, 128), F32),
            pltpu.VMEM((count * CHUNK, 128), F32),
        ],
        compiler_params=params(60),
        name="project_rest" if count == 3 else "project_own",
    )(*inputs)


def on_device(x, latents, rotary_keys, positions, wq, wk, wv, queries, owner, slot, cache, cache_rope, lengths):
    me = lax.axis_index("head").astype(jnp.int32).reshape(1)
    freq = jnp.asarray(ROPE_BASE ** (-np.arange(32) / 32.0), F32).reshape(32, 1)
    owner_row, slot_row = owner.reshape(1, ROWS), slot.reshape(1, ROWS)
    send = pl.pallas_call(
        place_kernel,
        out_shape=jax.ShapeDtypeStruct((PEERS * 2 * MOST, SEND), BF16),
        compiler_params=params(60),
        name="place",
    )(queries, owner_row, slot_row)
    recv = lax.all_to_all(send, "req", 0, 0, tiled=True)

    packed = pl.pallas_call(
        pack_kernel,
        in_specs=[whole((CHUNK, D_Q)), whole((CHUNK, D_C)), whole((64, CHUNK)), whole((1, CHUNK)), whole((32, 1)), anywhere()],
        out_specs=whole((CHUNK, PACK)),
        out_shape=jax.ShapeDtypeStruct((CHUNK, PACK), BF16),
        compiler_params=params(60),
        name="pack",
    )(x, latents, rotary_keys, positions.reshape(1, CHUNK), freq, send)
    right = lax.ppermute(packed, "head", [(i, (i + 3) % 4) for i in range(4)])
    left = lax.ppermute(packed, "head", [(i, (i + 1) % 4) for i in range(4)])
    far = lax.ppermute(packed, "head", [(i, (i + 2) % 4) for i in range(4)])
    own = project(1, project_own_kernel, (packed,), freq, wq, wk, wv, (), ())

    returned = pl.pallas_call(
        decode_kernel,
        grid=(SLOTS // SLOTS_PER_STEP,),
        in_specs=[
            whole((PEERS * 2 * MOST, SEND)),
            whole((D_C, HEADS * D_NOPE)),
            whole((D_C, HEADS * D_V)),
            pl.BlockSpec((SLOTS_PER_STEP, CMAX, D_C), lambda i: (i, 0, 0)),
            pl.BlockSpec((SLOTS_PER_STEP, D_ROPE, CMAX), lambda i: (i, 0, 0)),
            smem(),
            anywhere(),
        ],
        out_specs=whole((PEERS * 2 * MOST, RET)),
        out_shape=jax.ShapeDtypeStruct((PEERS * 2 * MOST, RET), BF16),
        scratch_shapes=[
            pltpu.VMEM((4, HEADS * SLOTS, 128), F32),
            pltpu.VMEM((HEADS * SLOTS, 128), F32),
            pltpu.VMEM((4, HEADS * SLOTS, 128), F32),
        ],
        compiler_params=params(60),
        name="decode",
    )(recv, wk, wv, cache, cache_rope, lengths, own[4])

    qn, qr, keys, values, key_rope = project(
        3, project_rest_kernel, (right, far, left), freq, wq, wk, wv, own, (returned,))
    returned = lax.all_to_all(returned, "req", 0, 0, tiled=True)

    prompt_out = pl.pallas_call(
        attention_kernel,
        grid=(HEADS // 2,),
        in_specs=[
            smem(),
            pl.BlockSpec((4, CHUNK, 256), lambda i: (0, 0, i)),
            pl.BlockSpec((4, CHUNK, 128), lambda i: (0, 0, i)),
            pl.BlockSpec((4, CHUNK, 256), lambda i: (0, 0, i)),
            pl.BlockSpec((4, CHUNK, 256), lambda i: (0, 0, i)),
            whole((4, CHUNK, 128)),
        ],
        out_specs=pl.BlockSpec((TOKENS, 256), lambda i: (0, i)),
        out_shape=jax.ShapeDtypeStruct((TOKENS, HEADS * D_V), BF16),
        scratch_shapes=[
            pltpu.VMEM((TOKENS, TOKENS), F32),
            pltpu.VMEM((2, 4, CHUNK, 128), BF16),
        ],
        compiler_params=params(60),
        name="attention",
    )(me, qn, qr, keys, values, key_rope)

    decode_out = pl.pallas_call(
        unplace_kernel,
        out_shape=jax.ShapeDtypeStruct((ROWS, HEADS * D_V), BF16),
        compiler_params=params(60),
        name="unplace",
    )(returned, owner_row)
    return prompt_out, decode_out


def solution(mesh):
    placed = (
        P(("req", "head"), None),
        P(("req", "head"), None),
        P(None, ("req", "head")),
        P(("req", "head")),
        P(None, "head"),
        P(None, "head"),
        P(None, "head"),
        P("req", "head"),
        P("req"),
        P("req"),
        P("req", None, None),
        P("req", None, None),
        P("req"),
    )
    return jax.shard_map(
        on_device,
        mesh=mesh,
        in_specs=placed,
        out_specs=(P("req", "head"), P("req", "head")),
        check_vma=False,
    )
```

```python
import math

import jax
import jax.numpy as jnp
import numpy as np
from jax import lax
from jax.experimental import pallas as pl
from jax.experimental.pallas import tpu as pltpu
from jax.sharding import PartitionSpec as P

D_C = 512
D_NOPE = 128
D_ROPE = 64
D_V = 128
D_Q = 1536
HEADS = 16
TOKENS = 512
CHUNK = 128
ROWS = 64
MOST = 4
SLOTS = 64
CMAX = 256
PEERS = 32
PACK = D_Q + D_C + 128
SEND = 1536 + 128
RET = 1024
ROPE_BASE = 10000.0
SCALE = (D_NOPE + D_ROPE) ** -0.5
SCALE_LOG2 = SCALE * math.log2(math.e)
MASKED = -1e30
F32 = jnp.float32
BF16 = jnp.bfloat16
MIB = 1024 * 1024


def iota(shape, dim):
    return lax.broadcasted_iota(jnp.int32, shape, dim)


def dot(a, b, dims=((1,), (0,))):
    return lax.dot_general(a, b, (dims, ((), ())), preferred_element_type=F32)


def column_of(row):
    n = row.shape[1]
    eye = iota((n, n), 0) == iota((n, n), 1)
    return jnp.sum(jnp.where(eye, row, 0), axis=1, keepdims=True)


def pack_kernel(x_ref, l_ref, rk_ref, pos_ref, freq_ref, len_ref, after_ref, packed_ref, order_ref, sorted_ref):
    packed_ref[:, :D_Q] = x_ref[...]
    packed_ref[:, D_Q:D_Q + D_C] = l_ref[...]
    pos = pos_ref[...]
    angle = pos.astype(F32) * freq_ref[...]
    cos, sin = jnp.cos(angle), jnp.sin(angle)
    keys = rk_ref[...].astype(F32)
    first, second = keys[:32], keys[32:]
    high = (pos >> 4).astype(F32)
    low = (pos & 15).astype(F32)
    place = iota((64, CHUNK), 0)
    tail = jnp.where(place == 0, high, jnp.where(place == 1, low, 0.0))
    block = jnp.concatenate([first * cos - second * sin, first * sin + second * cos, tail], axis=0)
    packed_ref[:, D_Q + D_C:] = block.T.astype(BF16)

    length = len_ref[...]
    length_col = column_of(length)
    this, other = iota((SLOTS, SLOTS), 0), iota((SLOTS, SLOTS), 1)
    ahead = (length < length_col) | ((length == length_col) & (other < this))
    rank = jnp.sum(jnp.where(ahead, 1, 0), axis=1, keepdims=True)
    order_ref[...] = jnp.sum(jnp.where(rank == other, this, 0), axis=0, keepdims=True)
    sorted_ref[...] = jnp.sum(jnp.where(rank == other, length_col, 0), axis=0, keepdims=True)


def place_kernel(q_ref, owner_ref, slot_ref, send_ref):
    owner = owner_ref[...]
    owner_col = column_of(owner)
    same = owner_col == owner
    before = iota((ROWS, ROWS), 0) < iota((ROWS, ROWS), 1)
    rank = jnp.sum(jnp.where(same & before, 1, 0), axis=0, keepdims=True)
    target = owner * (2 * MOST) + rank
    target = jnp.concatenate([target, target + MOST], axis=1)
    placing = iota((PEERS * 2 * MOST, 2 * ROWS), 0) == target
    queries = jnp.concatenate([q_ref[:, :1536], q_ref[:, 1536:]], axis=0)
    send_ref[:, :1536] = dot(placing.astype(BF16), queries).astype(BF16)
    slot = slot_ref[...] + 1
    slot = jnp.concatenate([slot, slot], axis=1)
    slot_col = jnp.sum(jnp.where(placing, slot, 0), axis=1, keepdims=True)
    send_ref[:, 1536:] = jnp.broadcast_to(slot_col.astype(F32), (PEERS * 2 * MOST, 128)).astype(BF16)


def split_pair(three):
    low_lane = iota((three.shape[0], 128), 1) < 64
    second, third = three[:, 128:256], three[:, 256:]
    rotary = jnp.where(low_lane, second, third)
    odd = pltpu.roll(jnp.where(low_lane, third, second), 64, 1)
    return three[:, :128], odd, rotary


TOGETHER = 8
WIDE = TOGETHER * HEADS
SECTION = 16
SECTIONS = SLOTS // SECTION
WIDTHS = (64, 128, 192, 256)


def decode_kernel(recv_hbm, kup_hbm, lat_hbm, rk_hbm, vup_hbm, order_ref, len_ref, order_row_ref, after_ref, out_ref,
                  recv_ref, kup_ref, lat_ref, rk_ref, vup_ref, lq_ref, qr_ref, lo_ref, sems, lat_sems):
    rows = PEERS * 2 * MOST
    copies = [pltpu.make_async_copy(src, dst, sems.at[i]) for i, (src, dst) in enumerate(
        ((recv_hbm, recv_ref), (kup_hbm, kup_ref), (rk_hbm, rk_ref), (vup_hbm, vup_ref)))]
    copies[0].start()
    copies[1].start()

    def of_width(section, width):
        longest = len_ref[section * SECTION + SECTION - 1]
        return (longest <= width) & (longest > width - 64)

    def fetch(section, width, place):
        return pltpu.make_async_copy(
            lat_hbm.at[order_ref[place], pl.ds(0, width)], lat_ref.at[place, pl.ds(0, width)], lat_sems.at[section])

    for section in range(SECTIONS):
        for width in WIDTHS:
            @pl.when(of_width(section, width))
            def _():
                @pl.loop(0, SECTION)
                def _(i):
                    fetch(section, width, section * SECTION + i).start()
        if section == 0:
            copies[2].start()
    copies[3].start()

    def place_onehot():
        slot_col = recv_ref[:, 1536:].astype(jnp.int32)
        hit = slot_col[:, :SLOTS] == order_row_ref[...] + 1
        half = (iota((rows, SLOTS), 0) & 7) < MOST
        return hit & half, hit & jnp.logical_not(half)

    copies[0].wait()
    first, second = place_onehot()
    blank = jnp.zeros((SLOTS, 128), BF16)
    low_lane = iota((SLOTS, 128), 1) < 64
    spreads = [jnp.concatenate([jnp.where(hit, 1.0, 0.0), jnp.zeros((rows, 64), F32)], axis=1).T[:SLOTS].astype(BF16)
               for hit in (first, second)]
    queries = [dot(spread, recv_ref[:, :1536]) for spread in spreads]
    copies[1].wait()
    for side in range(2):
        for pair in range(4):
            head = side * 8 + pair * 2
            even, odd, rotary = split_pair(queries[side][:, pair * 384:(pair + 1) * 384])
            both = jnp.concatenate([jnp.concatenate([even.astype(BF16), blank], axis=1),
                                    jnp.concatenate([blank, odd.astype(BF16)], axis=1)], axis=0)
            latent = dot(both, kup_ref[:, head * 128:(head + 2) * 128], ((1,), (1,)))
            lq_ref[head:head + 2] = latent.astype(BF16).astype(F32).reshape(2, SLOTS, D_C)
            turned = pltpu.roll(rotary, 64, 1)
            qr_ref[head] = jnp.where(low_lane, rotary, turned)
            qr_ref[head + 1] = jnp.where(low_lane, turned, rotary)
    copies[2].wait()

    def attend(section, width):
        @pl.loop(0, SECTION)
        def _(i):
            fetch(section, width, section * SECTION + i).wait()

        row, lane = iota((WIDE, WIDE), 0), iota((WIDE, WIDE), 1)
        by_place = jnp.where(lane == (row & 15) * TOGETHER + (row >> 4), 1.0, 0.0).astype(BF16)
        by_head = jnp.where(row == (lane & 15) * TOGETHER + (lane >> 4), 1.0, 0.0).astype(BF16)
        row_place = iota((WIDE, 1), 0) >> 4
        starts = [pl.multiple_of(section * SECTION + group * TOGETHER, TOGETHER) for group in range(SECTION // TOGETHER)]
        queries = []
        for start in starts:
            latent = lq_ref[:, pl.ds(start, TOGETHER), :].reshape(WIDE, D_C).astype(BF16)
            rotary = qr_ref[:, pl.ds(start, TOGETHER), :].reshape(WIDE, 128).astype(BF16)
            queries.append((dot(by_place, latent).astype(BF16), dot(by_place, rotary).astype(BF16)))
        scores = []
        for start, (latent, rotary) in zip(starts, queries):
            score = []
            length = jnp.full((WIDE, 1), len_ref[start], jnp.int32)
            for i in range(TOGETHER):
                mine = slice(i * HEADS, (i + 1) * HEADS)
                score.append(dot(latent[mine], lat_ref[start + i, :width], ((1,), (1,)))
                             + dot(rotary[mine, :D_ROPE], rk_ref[order_ref[start + i], :, :width]))
                length = jnp.where(row_place == i, len_ref[start + i], length)
            score = jnp.concatenate(score, axis=0)
            scores.append(jnp.where(iota((WIDE, width), 1) < length, score * SCALE, MASKED))
        for start, score in zip(starts, scores):
            raised = jnp.exp(score - jnp.max(score, axis=1, keepdims=True))
            weights = (raised * (1.0 / jnp.sum(raised, axis=1, keepdims=True))).astype(BF16)
            total = jnp.concatenate(
                [dot(weights[i * HEADS:(i + 1) * HEADS], lat_ref[start + i, :width]).astype(BF16)
                 for i in range(TOGETHER)], axis=0)
            lo_ref[:, pl.ds(start, TOGETHER), :] = dot(by_head, total).reshape(HEADS, TOGETHER, D_C)

    @pl.loop(0, SECTIONS)
    def _(section):
        for width in WIDTHS:
            @pl.when(of_width(section, width))
            def _():
                attend(section, width)

    copies[3].wait()
    outs = []
    for head in range(0, HEADS, 2):
        latent_out = lo_ref[head:head + 2].reshape(2 * SLOTS, D_C).astype(BF16)
        both = dot(latent_out, vup_ref[:, head * 128:(head + 2) * 128])
        outs += [both[:SLOTS, :128].astype(BF16), both[SLOTS:, 128:].astype(BF16)]
    outs = jnp.concatenate([jnp.concatenate(outs[:8], axis=1), jnp.concatenate(outs[8:], axis=1)], axis=0)
    first, second = place_onehot()
    spread = jnp.concatenate([jnp.where(first, 1.0, 0.0), jnp.where(second, 1.0, 0.0)], axis=1)
    out_ref[...] = dot(spread.astype(BF16), outs).astype(BF16)


def unplace_kernel(ret_ref, owner_ref, out_ref):
    owner = owner_ref[...]
    owner_col = column_of(owner)
    before = iota((ROWS, ROWS), 1) < iota((ROWS, ROWS), 0)
    rank = jnp.sum(jnp.where((owner_col == owner) & before, 1, 0), axis=1, keepdims=True)
    target = owner_col * (2 * MOST) + rank
    lane = iota((ROWS, PEERS * 2 * MOST), 1)
    for side in range(2):
        spread = jnp.where(lane == target + side * MOST, 1.0, 0.0).astype(BF16)
        out_ref[:, side * RET:(side + 1) * RET] = dot(spread, ret_ref[...]).astype(BF16)


GROUP = 4


def project_kernel(count, chunks, freq_ref, wq_ref, wk_ref, wv_ref, qn_ref, qr_ref, k_ref, v_ref, kr_ref,
                   x_ref, cos_ref, sin_ref):
    rows = count * CHUNK

    @pl.when(pl.program_id(0) == 0)
    def _():
        for i, chunk in enumerate(chunks):
            x_ref[i * CHUNK:(i + 1) * CHUNK, :] = chunk[...]
        extra = x_ref[:, D_Q + D_C:]
        kr_ref[...] = extra.reshape(count, CHUNK, 128)
        turned = extra.astype(F32).T
        pos = turned[64:65] * 16.0 + turned[65:66]
        angle = pos * freq_ref[...]
        cos, sin = jnp.cos(angle), jnp.sin(angle)
        cos_ref[...] = jnp.concatenate([cos, cos, cos, cos], axis=0).T
        sin_ref[...] = jnp.concatenate([-sin, sin, -sin, sin], axis=0).T

    lane = iota((rows, 128), 1) & 63
    shape = (count, CHUNK, 128)
    queries = dot(x_ref[:, :D_Q], wq_ref[...])
    for pair in range(GROUP // 2):
        even, odd, rotary = split_pair(queries[:, pair * 384:(pair + 1) * 384])
        qn_ref[:, :, pair * 256:pair * 256 + 128] = even.astype(BF16).reshape(shape)
        qn_ref[:, :, pair * 256 + 128:pair * 256 + 256] = odd.astype(BF16).reshape(shape)
        swapped = jnp.where(lane < 32, pltpu.roll(rotary, 96, 1), pltpu.roll(rotary, 32, 1))
        turned = (rotary * cos_ref[...] + swapped * sin_ref[...]).astype(BF16)
        qr_ref[:, :, pair * 128:(pair + 1) * 128] = turned.reshape(shape)
    latents = x_ref[:, D_Q:D_Q + D_C]
    k_ref[...] = dot(latents, wk_ref[...]).astype(BF16).reshape(count, CHUNK, GROUP * 128)
    v_ref[...] = dot(latents, wv_ref[...]).astype(BF16).reshape(count, CHUNK, GROUP * 128)


def project_own_kernel(own_ref, freq_ref, wq_ref, wk_ref, wv_ref, *rest):
    project_kernel(1, (own_ref,), freq_ref, wq_ref, wk_ref, wv_ref, *rest)


def project_rest_kernel(right_ref, far_ref, left_ref, freq_ref, wq_ref, wk_ref, wv_ref, a, b, c, d, e, after, *rest):
    project_kernel(3, (right_ref, far_ref, left_ref), freq_ref, wq_ref, wk_ref, wv_ref, *rest)


def attention_kernel(head_ref, qn_ref, qr_ref, k_ref, v_ref, kr_ref, out_ref, bias_ref, pair_ref):
    me = head_ref[0]
    place = [(c - me + 3) & 3 for c in range(4)]

    @pl.when(pl.program_id(0) == 0)
    def _():
        low_lane = iota((CHUNK, 128), 1) < 64
        for c in range(4):
            extra = kr_ref[place[c]].astype(F32)
            pos = (extra[:, 64:65] * 16.0 + extra[:, 65:66]).astype(jnp.int32)
            query, key = iota((CHUNK, TOKENS), 0) + c * CHUNK, iota((CHUNK, TOKENS), 1)
            bias_ref[c * CHUNK:(c + 1) * CHUNK, :] = jnp.where((key <= query) & (key >= query - pos), 0.0, MASKED)
            keep = jnp.where(low_lane, extra, 0.0)
            pair_ref[0, c] = keep.astype(BF16)
            pair_ref[1, c] = pltpu.roll(keep, 64, 1).astype(BF16)

    ones = jnp.ones((CHUNK, 128), BF16)
    half = TOKENS // 2
    scores = []
    for sub in range(2):
        lanes = slice(sub * 128, (sub + 1) * 128)
        query = [jnp.concatenate([qn_ref[place[c], :, lanes], qr_ref[place[c]]], axis=1) for c in range(4)]
        keys = [jnp.concatenate([k_ref[place[c], :, lanes], pair_ref[sub, c]], axis=1) for c in range(4)]
        early = dot(jnp.concatenate(query, axis=0), jnp.concatenate(keys[:2], axis=0), ((1,), (1,))) + bias_ref[:, :half]
        late = dot(jnp.concatenate(query[2:], axis=0), jnp.concatenate(keys[2:], axis=0), ((1,), (1,)))
        scores.append((early, late + bias_ref[half:, half:]))
    for sub in range(2):
        lanes = slice(sub * 128, (sub + 1) * 128)
        early, late = scores[sub]
        values = [jnp.concatenate([v_ref[place[c], :, lanes], ones], axis=1) for c in range(4)]
        top = jnp.max(early[:half], axis=1, keepdims=True)
        raised = jnp.exp2((early[:half] - top) * SCALE_LOG2).astype(BF16)
        top_late = jnp.max(jnp.maximum(early[half:], late), axis=1, keepdims=True)
        raised_late = [jnp.exp2((part - top_late) * SCALE_LOG2).astype(BF16) for part in (early[half:], late)]
        total = dot(jnp.concatenate([raised, raised_late[0]], axis=0), jnp.concatenate(values[:2], axis=0))
        total_late = total[half:] + dot(raised_late[1], jnp.concatenate(values[2:], axis=0))
        out_ref[:half, lanes] = (total[:half, :128] / total[:half, 128:]).astype(BF16)
        out_ref[half:, lanes] = (total_late[:, :128] / total_late[:, 128:]).astype(BF16)


def whole(shape):
    return pl.BlockSpec(shape, lambda *_: (0,) * len(shape))


def params(mib):
    return pltpu.CompilerParams(vmem_limit_bytes=mib * MIB)


def smem():
    return pl.BlockSpec(memory_space=pltpu.SMEM)


def anywhere():
    return pl.BlockSpec(memory_space=pl.ANY)


def project(count, kernel, chunks, freq, wq, wk, wv, into, after):
    first = 0 if into else 3
    shapes = [(HEADS * 128, GROUP * 128), (HEADS * 64, GROUP * 64), (HEADS * 128, GROUP * 128), (HEADS * 128, GROUP * 128)]
    inputs = list(chunks) + [freq, wq, wk, wv] + list(into) + list(after)
    n = len(chunks) + 4
    return pl.pallas_call(
        kernel,
        grid=(HEADS // GROUP,),
        in_specs=[whole((CHUNK, PACK))] * len(chunks) + [
            whole((32, 1)),
            pl.BlockSpec((D_Q, GROUP * 192), lambda i: (0, i)),
            pl.BlockSpec((D_C, GROUP * 128), lambda i: (0, i)),
            pl.BlockSpec((D_C, GROUP * 128), lambda i: (0, i)),
        ] + [anywhere()] * (len(into) + len(after)),
        out_specs=[pl.BlockSpec((count, CHUNK, block), lambda i: (first, 0, i)) for _, block in shapes]
        + [pl.BlockSpec((count, CHUNK, 128), lambda i: (first, 0, 0))],
        out_shape=[jax.ShapeDtypeStruct((4, CHUNK, width), BF16) for width, _ in shapes]
        + [jax.ShapeDtypeStruct((4, CHUNK, 128), BF16)],
        input_output_aliases={n + i: i for i in range(len(into))},
        scratch_shapes=[
            pltpu.VMEM((count * CHUNK, PACK), BF16),
            pltpu.VMEM((count * CHUNK, 128), F32),
            pltpu.VMEM((count * CHUNK, 128), F32),
        ],
        compiler_params=params(60),
        name="project_rest" if count == 3 else "project_own",
    )(*inputs)


def on_device(x, latents, rotary_keys, positions, wq, wk, wv, queries, owner, slot, cache, cache_rope, lengths):
    me = lax.axis_index("head").astype(jnp.int32).reshape(1)
    freq = jnp.asarray(ROPE_BASE ** (-np.arange(32) / 32.0), F32).reshape(32, 1)
    owner_row, slot_row = owner.reshape(1, ROWS), slot.reshape(1, ROWS)
    send = pl.pallas_call(
        place_kernel,
        out_shape=jax.ShapeDtypeStruct((PEERS * 2 * MOST, SEND), BF16),
        compiler_params=params(60),
        name="place",
    )(queries, owner_row, slot_row)
    recv = lax.all_to_all(send, "req", 0, 0, tiled=True)

    row = jax.ShapeDtypeStruct((1, SLOTS), jnp.int32)
    packed, order, ordered_lengths = pl.pallas_call(
        pack_kernel,
        in_specs=[whole((CHUNK, D_Q)), whole((CHUNK, D_C)), whole((64, CHUNK)), whole((1, CHUNK)), whole((32, 1)),
                  whole((1, SLOTS)), anywhere()],
        out_specs=[whole((CHUNK, PACK)), whole((1, SLOTS)), whole((1, SLOTS))],
        out_shape=[jax.ShapeDtypeStruct((CHUNK, PACK), BF16), row, row],
        compiler_params=params(60),
        name="pack",
    )(x, latents, rotary_keys, positions.reshape(1, CHUNK), freq, lengths.reshape(1, SLOTS), send)
    right = lax.ppermute(packed, "head", [(i, (i + 3) % 4) for i in range(4)])
    left = lax.ppermute(packed, "head", [(i, (i + 1) % 4) for i in range(4)])
    far = lax.ppermute(packed, "head", [(i, (i + 2) % 4) for i in range(4)])
    own = project(1, project_own_kernel, (packed,), freq, wq, wk, wv, (), ())

    returned = pl.pallas_call(
        decode_kernel,
        in_specs=[anywhere()] * 5 + [smem(), smem(), whole((1, SLOTS)), anywhere()],
        out_specs=whole((PEERS * 2 * MOST, RET)),
        out_shape=jax.ShapeDtypeStruct((PEERS * 2 * MOST, RET), BF16),
        scratch_shapes=[
            pltpu.VMEM((PEERS * 2 * MOST, SEND), BF16),
            pltpu.VMEM((D_C, HEADS * D_NOPE), BF16),
            pltpu.VMEM((SLOTS, CMAX, D_C), BF16),
            pltpu.VMEM((SLOTS, D_ROPE, CMAX), BF16),
            pltpu.VMEM((D_C, HEADS * D_V), BF16),
            pltpu.VMEM((HEADS, SLOTS, D_C), F32),
            pltpu.VMEM((HEADS, SLOTS, 128), F32),
            pltpu.VMEM((HEADS, SLOTS, D_C), F32),
            pltpu.SemaphoreType.DMA((4,)),
            pltpu.SemaphoreType.DMA((SECTIONS,)),
        ],
        compiler_params=params(60),
        name="decode",
    )(recv, wk, cache, cache_rope, wv, order.reshape(SLOTS), ordered_lengths.reshape(SLOTS), order, own[4])

    qn, qr, keys, values, key_rope = project(
        3, project_rest_kernel, (right, far, left), freq, wq, wk, wv, own, (returned,))
    returned = lax.all_to_all(returned, "req", 0, 0, tiled=True)

    prompt_out = pl.pallas_call(
        attention_kernel,
        grid=(HEADS // 2,),
        in_specs=[
            smem(),
            pl.BlockSpec((4, CHUNK, 256), lambda i: (0, 0, i)),
            pl.BlockSpec((4, CHUNK, 128), lambda i: (0, 0, i)),
            pl.BlockSpec((4, CHUNK, 256), lambda i: (0, 0, i)),
            pl.BlockSpec((4, CHUNK, 256), lambda i: (0, 0, i)),
            whole((4, CHUNK, 128)),
        ],
        out_specs=pl.BlockSpec((TOKENS, 256), lambda i: (0, i)),
        out_shape=jax.ShapeDtypeStruct((TOKENS, HEADS * D_V), BF16),
        scratch_shapes=[
            pltpu.VMEM((TOKENS, TOKENS), F32),
            pltpu.VMEM((2, 4, CHUNK, 128), BF16),
        ],
        compiler_params=params(60),
        name="attention",
    )(me, qn, qr, keys, values, key_rope)

    decode_out = pl.pallas_call(
        unplace_kernel,
        out_shape=jax.ShapeDtypeStruct((ROWS, HEADS * D_V), BF16),
        compiler_params=params(60),
        name="unplace",
    )(returned, owner_row)
    return prompt_out, decode_out


def solution(mesh):
    placed = (
        P(("req", "head"), None),
        P(("req", "head"), None),
        P(None, ("req", "head")),
        P(("req", "head")),
        P(None, "head"),
        P(None, "head"),
        P(None, "head"),
        P("req", "head"),
        P("req"),
        P("req"),
        P("req", None, None),
        P("req", None, None),
        P("req"),
    )
    return jax.shard_map(
        on_device,
        mesh=mesh,
        in_specs=placed,
        out_specs=(P("req", "head"), P("req", "head")),
        check_vma=False,
    )
```

```python
import math

import jax
import jax.numpy as jnp
from jax import lax
from jax.experimental import pallas as pl
from jax.experimental.pallas import tpu as pltpu
from jax.sharding import PartitionSpec as P

D_C = 512
D_NOPE = 128
D_ROPE = 64
D_V = 128
D_Q = 1536
HEADS = 16
TOKENS = 512
CHUNK = 128
ROWS = 64
MOST = 4
SLOTS = 64
CMAX = 256
PEERS = 32
PACK = D_Q + D_C + 128
SEND = 1536 + 128
RET = 1024
ROPE_BASE = 10000.0
SCALE = (D_NOPE + D_ROPE) ** -0.5
SCALE_LOG2 = SCALE * math.log2(math.e)
MASKED = -1e30
F32 = jnp.float32
BF16 = jnp.bfloat16
MIB = 1024 * 1024


def iota(shape, dim):
    return lax.broadcasted_iota(jnp.int32, shape, dim)


def dot(a, b, dims=((1,), (0,))):
    return lax.dot_general(a, b, (dims, ((), ())), preferred_element_type=F32)


def frequencies():
    return jnp.exp(iota((32, 128), 0).astype(F32) * (-math.log(ROPE_BASE) / 32.0))[:, :1]


def column_of(row):
    n = row.shape[1]
    eye = iota((n, n), 0) == iota((n, n), 1)
    return jnp.sum(jnp.where(eye, row, 0), axis=1, keepdims=True)


def pack_kernel(x_ref, l_ref, rk_ref, pos_ref, len_ref, after_ref, packed_ref, order_ref, sorted_ref):
    packed_ref[:, :D_Q] = x_ref[...]
    packed_ref[:, D_Q:D_Q + D_C] = l_ref[...]
    pos = pos_ref[...]
    angle = pos.astype(F32) * frequencies()
    cos, sin = jnp.cos(angle), jnp.sin(angle)
    keys = rk_ref[...].astype(F32)
    first, second = keys[:32], keys[32:]
    high = (pos >> 4).astype(F32)
    low = (pos & 15).astype(F32)
    place = iota((64, CHUNK), 0)
    tail = jnp.where(place == 0, high, jnp.where(place == 1, low, 0.0))
    block = jnp.concatenate([first * cos - second * sin, first * sin + second * cos, tail], axis=0)
    packed_ref[:, D_Q + D_C:] = block.T.astype(BF16)

    length = len_ref[...]
    length_col = column_of(length)
    this, other = iota((SLOTS, SLOTS), 0), iota((SLOTS, SLOTS), 1)
    ahead = (length < length_col) | ((length == length_col) & (other < this))
    rank = jnp.sum(jnp.where(ahead, 1, 0), axis=1, keepdims=True)
    order_ref[...] = jnp.sum(jnp.where(rank == other, this, 0), axis=0, keepdims=True)
    sorted_ref[...] = jnp.sum(jnp.where(rank == other, length_col, 0), axis=0, keepdims=True)


def place_kernel(q_ref, owner_ref, slot_ref, send_ref):
    owner = owner_ref[...]
    owner_col = column_of(owner)
    same = owner_col == owner
    before = iota((ROWS, ROWS), 0) < iota((ROWS, ROWS), 1)
    rank = jnp.sum(jnp.where(same & before, 1, 0), axis=0, keepdims=True)
    target = owner * (2 * MOST) + rank
    target = jnp.concatenate([target, target + MOST], axis=1)
    placing = iota((PEERS * 2 * MOST, 2 * ROWS), 0) == target
    queries = jnp.concatenate([q_ref[:, :1536], q_ref[:, 1536:]], axis=0)
    send_ref[:, :1536] = dot(placing.astype(BF16), queries).astype(BF16)
    slot = slot_ref[...] + 1
    slot = jnp.concatenate([slot, slot], axis=1)
    slot_col = jnp.sum(jnp.where(placing, slot, 0), axis=1, keepdims=True)
    send_ref[:, 1536:] = jnp.broadcast_to(slot_col.astype(F32), (PEERS * 2 * MOST, 128)).astype(BF16)


def split_pair(three):
    low_lane = iota((three.shape[0], 128), 1) < 64
    second, third = three[:, 128:256], three[:, 256:]
    rotary = jnp.where(low_lane, second, third)
    odd = pltpu.roll(jnp.where(low_lane, third, second), 64, 1)
    return three[:, :128], odd, rotary


TOGETHER = 8
WIDE = TOGETHER * HEADS
SECTION = 16
SECTIONS = SLOTS // SECTION
WIDTHS = (64, 128, 192, 256)


def decode_kernel(recv_ref, kup_hbm, lat_hbm, rk_hbm, vup_hbm, order_hbm, order_ref, len_ref, after_ref, out_ref,
                  kup_ref, rk_ref, vup_ref, order_row_ref, lat_ref, lq_ref, qr_ref, lo_ref, sems, lat_sems):
    rows = PEERS * 2 * MOST
    order_copy, kup_copy, rk_copy, vup_copy = [
        pltpu.make_async_copy(src, dst, sems.at[i]) for i, (src, dst) in enumerate(
            ((order_hbm, order_row_ref), (kup_hbm, kup_ref), (rk_hbm, rk_ref), (vup_hbm, vup_ref)))]

    def of_width(section, width):
        longest = len_ref[section * SECTION + SECTION - 1]
        return (longest <= width) & (longest > width - 64)

    def fetch(section, width, i):
        place = section * SECTION + i
        return pltpu.make_async_copy(
            lat_hbm.at[order_ref[place], pl.ds(0, width)], lat_ref.at[place, pl.ds(0, width)], lat_sems.at[section])

    def start(section):
        for width in WIDTHS:
            @pl.when(of_width(section, width))
            def _():
                for i in range(SECTION):
                    fetch(section, width, i).start()

    order_copy.start()
    kup_copy.start()
    start(0)
    rk_copy.start()

    def place_onehot():
        slot_col = recv_ref[:, 1536:].astype(jnp.int32)
        hit = slot_col[:, :SLOTS] == order_row_ref[...] + 1
        half = (iota((rows, SLOTS), 0) & 7) < MOST
        return hit & half, hit & jnp.logical_not(half)

    order_copy.wait()
    first, second = place_onehot()
    blank = jnp.zeros((SLOTS, 128), BF16)
    low_lane = iota((SLOTS, 128), 1) < 64
    spreads = [jnp.concatenate([jnp.where(hit, 1.0, 0.0), jnp.zeros((rows, 64), F32)], axis=1).T[:SLOTS].astype(BF16)
               for hit in (first, second)]
    queries = [dot(spread, recv_ref[:, :1536]) for spread in spreads]
    kup_copy.wait()
    start(1)
    for side in range(2):
        for pair in range(4):
            head = side * 8 + pair * 2
            even, odd, rotary = split_pair(queries[side][:, pair * 384:(pair + 1) * 384])
            both = jnp.concatenate([jnp.concatenate([even.astype(BF16), blank], axis=1),
                                    jnp.concatenate([blank, odd.astype(BF16)], axis=1)], axis=0)
            latent = dot(both, kup_ref[:, head * 128:(head + 2) * 128], ((1,), (1,)))
            lq_ref[head:head + 2] = latent.astype(BF16).astype(F32).reshape(2, SLOTS, D_C)
            turned = pltpu.roll(rotary, 64, 1)
            qr_ref[head] = jnp.where(low_lane, rotary, turned)
            qr_ref[head + 1] = jnp.where(low_lane, turned, rotary)
    rk_copy.wait()
    start(2)

    def attend(section, width):
        @pl.loop(0, SECTION)
        def _(i):
            fetch(section, width, i).wait()

        row, lane = iota((WIDE, WIDE), 0), iota((WIDE, WIDE), 1)
        by_place = jnp.where(lane == (row & 15) * TOGETHER + (row >> 4), 1.0, 0.0).astype(BF16)
        by_head = jnp.where(row == (lane & 15) * TOGETHER + (lane >> 4), 1.0, 0.0).astype(BF16)
        row_place = iota((WIDE, 1), 0) >> 4
        starts = [pl.multiple_of(section * SECTION + group * TOGETHER, TOGETHER) for group in range(SECTION // TOGETHER)]
        queries = []
        for start in starts:
            latent = lq_ref[:, pl.ds(start, TOGETHER), :].reshape(WIDE, D_C).astype(BF16)
            rotary = qr_ref[:, pl.ds(start, TOGETHER), :].reshape(WIDE, 128).astype(BF16)
            queries.append((dot(by_place, latent).astype(BF16), dot(by_place, rotary).astype(BF16)))
        scores = []
        for start, (latent, rotary) in zip(starts, queries):
            score = []
            length = jnp.full((WIDE, 1), len_ref[start], jnp.int32)
            for i in range(TOGETHER):
                mine = slice(i * HEADS, (i + 1) * HEADS)
                score.append(dot(latent[mine], lat_ref[start + i, :width], ((1,), (1,)))
                             + dot(rotary[mine, :D_ROPE], rk_ref[order_ref[start + i], :, :width]))
                length = jnp.where(row_place == i, len_ref[start + i], length)
            score = jnp.concatenate(score, axis=0)
            scores.append(jnp.where(iota((WIDE, width), 1) < length, score * SCALE, MASKED))
        for start, score in zip(starts, scores):
            raised = jnp.exp(score - jnp.max(score, axis=1, keepdims=True))
            weights = (raised * (1.0 / jnp.sum(raised, axis=1, keepdims=True))).astype(BF16)
            total = jnp.concatenate(
                [dot(weights[i * HEADS:(i + 1) * HEADS], lat_ref[start + i, :width]).astype(BF16)
                 for i in range(TOGETHER)], axis=0)
            lo_ref[:, pl.ds(start, TOGETHER), :] = dot(by_head, total).reshape(HEADS, TOGETHER, D_C)

    @pl.loop(0, SECTIONS)
    def _(section):
        @pl.when(section == 0)
        def _():
            start(SECTIONS - 1)
            vup_copy.start()

        for width in WIDTHS:
            @pl.when(of_width(section, width))
            def _():
                attend(section, width)

    vup_copy.wait()
    outs = []
    for head in range(0, HEADS, 2):
        latent_out = lo_ref[head:head + 2].reshape(2 * SLOTS, D_C).astype(BF16)
        both = dot(latent_out, vup_ref[:, head * 128:(head + 2) * 128])
        outs += [both[:SLOTS, :128].astype(BF16), both[SLOTS:, 128:].astype(BF16)]
    outs = jnp.concatenate([jnp.concatenate(outs[:8], axis=1), jnp.concatenate(outs[8:], axis=1)], axis=0)
    first, second = place_onehot()
    spread = jnp.concatenate([jnp.where(first, 1.0, 0.0), jnp.where(second, 1.0, 0.0)], axis=1)
    out_ref[...] = dot(spread.astype(BF16), outs).astype(BF16)


def unplace_kernel(ret_ref, owner_ref, out_ref):
    owner = owner_ref[...]
    owner_col = column_of(owner)
    before = iota((ROWS, ROWS), 1) < iota((ROWS, ROWS), 0)
    rank = jnp.sum(jnp.where((owner_col == owner) & before, 1, 0), axis=1, keepdims=True)
    target = owner_col * (2 * MOST) + rank
    lane = iota((ROWS, PEERS * 2 * MOST), 1)
    for side in range(2):
        spread = jnp.where(lane == target + side * MOST, 1.0, 0.0).astype(BF16)
        out_ref[:, side * RET:(side + 1) * RET] = dot(spread, ret_ref[...]).astype(BF16)


GROUP = 4


GROUPS = HEADS // GROUP


def fetch_weights(group, sources, buffers, sems):
    return [pltpu.make_async_copy(
        src.at[:, pl.ds(pl.multiple_of(group * width, 128), width)], dst.at[group], sems.at[i, group])
        for i, (src, dst, width) in enumerate(zip(sources, buffers, (GROUP * 192, GROUP * 128, GROUP * 128)))]


def rope_tables(extra):
    turned = extra.astype(F32).T
    pos = turned[64:65] * 16.0 + turned[65:66]
    angle = pos * frequencies()
    cos, sin = jnp.cos(angle), jnp.sin(angle)
    return (jnp.concatenate([cos, cos, cos, cos], axis=0).T, jnp.concatenate([-sin, sin, -sin, sin], axis=0).T)


def rotated(rotary, cos, sin):
    lane = iota(rotary.shape, 1) & 63
    swapped = jnp.where(lane < 32, pltpu.roll(rotary, 96, 1), pltpu.roll(rotary, 32, 1))
    return (rotary * cos + swapped * sin).astype(BF16)


def own_kernel(x_ref, wq_hbm, wk_hbm, wv_hbm,
               qn_ref, qr_ref, k_ref, v_ref, wq_ref, wk_ref, wv_ref, cos_ref, sin_ref, sems):
    def fetch(group):
        return fetch_weights(group, (wq_hbm, wk_hbm, wv_hbm), (wq_ref, wk_ref, wv_ref), sems)

    for group in range(GROUPS):
        for copy in fetch(group):
            copy.start()
    cos_ref[...], sin_ref[...] = rope_tables(x_ref[:, D_Q + D_C:])

    @pl.loop(0, GROUPS)
    def _(group):
        for copy in fetch(group):
            copy.wait()
        queries = dot(x_ref[:, :D_Q], wq_ref[group])
        for pair in range(GROUP // 2):
            even, odd, rotary = split_pair(queries[:, pair * 384:(pair + 1) * 384])
            qn_ref[group, :, pair * 256:pair * 256 + 128] = even.astype(BF16)
            qn_ref[group, :, pair * 256 + 128:pair * 256 + 256] = odd.astype(BF16)
            qr_ref[group, :, pair * 128:(pair + 1) * 128] = rotated(rotary, cos_ref[...], sin_ref[...])
        latents = x_ref[:, D_Q:D_Q + D_C]
        k_ref[group] = dot(latents, wk_ref[group]).astype(BF16)
        v_ref[group] = dot(latents, wv_ref[group]).astype(BF16)


def prefill_kernel(head_ref, right_ref, far_ref, left_ref, own_hbm, wq_hbm, wk_hbm, wv_hbm,
                   own_qn_hbm, own_qr_hbm, own_k_hbm, own_v_hbm, after_ref, out_hbm,
                   own_ref, all_wq_ref, all_wk_ref, all_wv_ref, all_out_ref, chunk_sem, weight_sems, own_sems, out_sems,
                   cos_ref, sin_ref, bias_ref, pair_ref, *sets):
    me = head_ref[0]
    place = [(c - me + 3) & 3 for c in range(4)]
    half = TOKENS // 2
    sets = (sets[:4], sets[4:])
    others = (right_ref, far_ref, left_ref)
    shared_copy = pltpu.make_async_copy(own_hbm.at[:, pl.ds(D_Q + D_C, 128)], own_ref, chunk_sem)

    def fetch(group):
        return fetch_weights(group, (wq_hbm, wk_hbm, wv_hbm), (all_wq_ref, all_wk_ref, all_wv_ref), weight_sems)

    def fetch_own(group, into, parity):
        return [pltpu.make_async_copy(src.at[group], dst.at[3], own_sems.at[i, parity])
                for i, (src, dst) in enumerate(zip((own_qn_hbm, own_qr_hbm, own_k_hbm, own_v_hbm), into))]

    def send_out(group):
        return pltpu.make_async_copy(
            all_out_ref.at[group], out_hbm.at[:, pl.ds(pl.multiple_of(group * GROUP * 128, 128), GROUP * 128)],
            out_sems.at[group])

    def prepare():
        extras = [ref[:, D_Q + D_C:] for ref in others] + [own_ref[...]]
        cos_ref[...], sin_ref[...] = rope_tables(jnp.concatenate(extras[:3], axis=0))
        low_lane = iota((CHUNK, 128), 1) < 64
        for slot, extra in enumerate(extras):
            extra = extra.astype(F32)
            pos = (extra[:, 64:65] * 16.0 + extra[:, 65:66]).astype(jnp.int32)
            chunk = (slot + 1 + me) & 3
            query, key = iota((CHUNK, TOKENS), 0) + chunk * CHUNK, iota((CHUNK, TOKENS), 1)
            bias_ref[chunk] = jnp.where((key <= query) & (key >= query - pos), 0.0, MASKED)
            keep = jnp.where(low_lane, extra, 0.0)
            pair_ref[0, chunk] = keep.astype(BF16)
            pair_ref[1, chunk] = pltpu.roll(keep, 64, 1).astype(BF16)

    def project_steps(into, group):
        qn_ref, qr_ref, k_ref, v_ref = into
        wq_ref, wk_ref, wv_ref = all_wq_ref.at[group], all_wk_ref.at[group], all_wv_ref.at[group]
        rows = 3 * CHUNK
        shape = (3, CHUNK, 128)
        held = []

        def query(first, width):
            x = jnp.concatenate([ref[:, :D_Q] for ref in others], axis=0)
            held.append(dot(x, wq_ref[:, first:first + width]))

        def turn(pair):
            even, odd, rotary = split_pair(jnp.concatenate(held, axis=1)[:, pair * 384:(pair + 1) * 384])
            qn_ref[:3, :, pair * 256:pair * 256 + 128] = even.astype(BF16).reshape(shape)
            qn_ref[:3, :, pair * 256 + 128:pair * 256 + 256] = odd.astype(BF16).reshape(shape)
            qr_ref[:3, :, pair * 128:(pair + 1) * 128] = rotated(rotary, cos_ref[...], sin_ref[...]).reshape(shape)

        def latent(which):
            w_ref, to_ref = ((wk_ref, k_ref), (wv_ref, v_ref))[which - 1]
            x = jnp.concatenate([ref[:, D_Q:D_Q + D_C] for ref in others], axis=0)
            to_ref[:3] = dot(x, w_ref[...]).astype(BF16).reshape(3, CHUNK, GROUP * 128)

        return query, turn, latent

    def attend_steps(source, group):
        qn_ref, qr_ref, k_ref, v_ref = source
        out_ref = all_out_ref.at[group]
        ones = jnp.ones((CHUNK, 128), BF16)
        scores = {}

        def score(head):
            lanes = slice(head * 128, (head + 1) * 128)
            pair = slice(head // 2 * 128, (head // 2 + 1) * 128)
            query = [jnp.concatenate([qn_ref[place[c], :, lanes], qr_ref[place[c], :, pair]], axis=1) for c in range(4)]
            keys = [jnp.concatenate([k_ref[place[c], :, lanes], pair_ref[head % 2, c]], axis=1) for c in range(4)]
            bias = bias_ref[...].reshape(TOKENS, TOKENS)
            early = dot(jnp.concatenate(query, axis=0), jnp.concatenate(keys[:2], axis=0), ((1,), (1,)))
            late = dot(jnp.concatenate(query[2:], axis=0), jnp.concatenate(keys[2:], axis=0), ((1,), (1,)))
            scores[head] = early + bias[:, :half], late + bias[half:, half:]

        def weigh(head):
            lanes = slice(head * 128, (head + 1) * 128)
            early, late = scores[head]
            values = [jnp.concatenate([v_ref[place[c], :, lanes], ones], axis=1) for c in range(4)]
            top = jnp.max(early[:half], axis=1, keepdims=True)
            raised = jnp.exp2((early[:half] - top) * SCALE_LOG2).astype(BF16)
            top_late = jnp.max(jnp.maximum(early[half:], late), axis=1, keepdims=True)
            raised_late = [jnp.exp2((part - top_late) * SCALE_LOG2).astype(BF16) for part in (early[half:], late)]
            total = dot(jnp.concatenate([raised, raised_late[0]], axis=0), jnp.concatenate(values[:2], axis=0))
            total_late = total[half:] + dot(raised_late[1], jnp.concatenate(values[2:], axis=0))
            out_ref[:half, lanes] = (total[:half, :128] / total[:half, 128:]).astype(BF16)
            out_ref[half:, lanes] = (total_late[:, :128] / total_late[:, 128:]).astype(BF16)

        return score, weigh

    def step_copies(copies, act):
        for copy in copies:
            act(copy)

    start, wait = (lambda copy: copy.start()), (lambda copy: copy.wait())
    shared_copy.start()
    step_copies(fetch(0), start)
    shared_copy.wait()
    prepare()
    step_copies(fetch(0), wait)
    step_copies(fetch(1), start)
    step_copies(fetch_own(0, sets[0], 0), start)
    query, turn, latent = project_steps(sets[0], 0)
    query(0, 512)
    query(512, 256)
    turn(0)
    latent(1)
    turn(1)
    latent(2)

    @pl.loop(1, GROUPS)
    def _(step):
        step_copies(fetch(step), wait)

        @pl.when(step < GROUPS - 1)
        def _():
            step_copies(fetch(step + 1), start)

        for parity in range(2):
            @pl.when((step & 1) == parity)
            def _():
                source, into = sets[1 - parity], sets[parity]
                step_copies(fetch_own(step, into, parity), start)
                step_copies(fetch_own(step - 1, source, 1 - parity), wait)
                score, weigh = attend_steps(source, step - 1)
                query, turn, latent = project_steps(into, step)
                score(0)
                query(0, 512)
                score(1)
                weigh(0)
                query(512, 256)
                turn(0)
                score(2)
                weigh(1)
                latent(1)
                turn(1)
                score(3)
                weigh(2)
                latent(2)
                weigh(3)
        send_out(step - 1).start()

    last = GROUPS - 1
    step_copies(fetch_own(last, sets[last % 2], last % 2), wait)
    score, weigh = attend_steps(sets[last % 2], last)
    score(0)
    for head in range(GROUP):
        if head + 1 < GROUP:
            score(head + 1)
        weigh(head)
    send_out(last).start()
    for group in range(GROUPS):
        send_out(group).wait()


def whole(shape):
    return pl.BlockSpec(shape, lambda *_: (0,) * len(shape))


def params(mib):
    return pltpu.CompilerParams(vmem_limit_bytes=mib * MIB)


def smem():
    return pl.BlockSpec(memory_space=pltpu.SMEM)


def anywhere():
    return pl.BlockSpec(memory_space=pl.ANY)


def vmem():
    return pl.BlockSpec(memory_space=pltpu.VMEM)


SETS = (GROUP * 128, GROUP * 64, GROUP * 128, GROUP * 128)


WEIGHTS = [pltpu.VMEM((GROUPS, D_Q, GROUP * 192), BF16), pltpu.VMEM((GROUPS, D_C, GROUP * 128), BF16),
           pltpu.VMEM((GROUPS, D_C, GROUP * 128), BF16)]


def project_own(packed, wq, wk, wv):
    return pl.pallas_call(
        own_kernel,
        in_specs=[vmem(), anywhere(), anywhere(), anywhere()],
        out_specs=[vmem()] * 4,
        out_shape=[jax.ShapeDtypeStruct((GROUPS, CHUNK, width), BF16) for width in SETS],
        scratch_shapes=WEIGHTS + [
            pltpu.VMEM((CHUNK, 128), F32),
            pltpu.VMEM((CHUNK, 128), F32),
            pltpu.SemaphoreType.DMA((3, GROUPS)),
        ],
        compiler_params=params(60),
        name="own",
    )(packed, wq, wk, wv)


def prefill(me, right, far, left, packed, wq, wk, wv, own, after):
    return pl.pallas_call(
        prefill_kernel,
        in_specs=[smem()] + [vmem()] * 3 + [anywhere()] * 9,
        out_specs=anywhere(),
        out_shape=jax.ShapeDtypeStruct((TOKENS, HEADS * D_V), BF16),
        scratch_shapes=[pltpu.VMEM((CHUNK, 128), BF16)] + WEIGHTS + [
            pltpu.VMEM((GROUPS, TOKENS, GROUP * 128), BF16),
            pltpu.SemaphoreType.DMA,
            pltpu.SemaphoreType.DMA((3, GROUPS)),
            pltpu.SemaphoreType.DMA((4, 2)),
            pltpu.SemaphoreType.DMA((GROUPS,)),
            pltpu.VMEM((3 * CHUNK, 128), F32),
            pltpu.VMEM((3 * CHUNK, 128), F32),
            pltpu.VMEM((4, CHUNK, TOKENS), F32),
            pltpu.VMEM((2, 4, CHUNK, 128), BF16),
        ] + [pltpu.VMEM((4, CHUNK, width), BF16) for width in SETS] * 2,
        compiler_params=params(36),
        name="prefill",
    )(me, right, far, left, pltpu.with_memory_space_constraint(packed, pltpu.HBM), wq, wk, wv,
      *(pltpu.with_memory_space_constraint(part, pltpu.HBM) for part in own), after)


def on_device(x, latents, rotary_keys, positions, wq, wk, wv, queries, owner, slot, cache, cache_rope, lengths):
    me = lax.axis_index("head").astype(jnp.int32).reshape(1)
    wq, wk, wv, cache, cache_rope = (
        pltpu.with_memory_space_constraint(array, pltpu.HBM) for array in (wq, wk, wv, cache, cache_rope))
    owner_row, slot_row = owner.reshape(1, ROWS), slot.reshape(1, ROWS)
    send = pl.pallas_call(
        place_kernel,
        out_shape=jax.ShapeDtypeStruct((PEERS * 2 * MOST, SEND), BF16),
        compiler_params=params(60),
        name="place",
    )(queries, owner_row, slot_row)
    recv = lax.all_to_all(send, "req", 0, 0, tiled=True)

    row = jax.ShapeDtypeStruct((1, SLOTS), jnp.int32)
    packed, order, ordered_lengths = pl.pallas_call(
        pack_kernel,
        in_specs=[whole((CHUNK, D_Q)), whole((CHUNK, D_C)), whole((64, CHUNK)), whole((1, CHUNK)), whole((1, SLOTS)), anywhere()],
        out_specs=[whole((CHUNK, PACK)), whole((1, SLOTS)), whole((1, SLOTS))],
        out_shape=[jax.ShapeDtypeStruct((CHUNK, PACK), BF16), row, row],
        compiler_params=params(60),
        name="pack",
    )(x, latents, rotary_keys, positions.reshape(1, CHUNK), lengths.reshape(1, SLOTS), send)
    right = lax.ppermute(packed, "head", [(i, (i + 3) % 4) for i in range(4)])
    left = lax.ppermute(packed, "head", [(i, (i + 1) % 4) for i in range(4)])
    far = lax.ppermute(packed, "head", [(i, (i + 2) % 4) for i in range(4)])
    own = project_own(packed, wq, wk, wv)

    returned = pl.pallas_call(
        decode_kernel,
        in_specs=[vmem()] + [anywhere()] * 5 + [smem(), smem(), anywhere()],
        out_specs=whole((PEERS * 2 * MOST, RET)),
        out_shape=jax.ShapeDtypeStruct((PEERS * 2 * MOST, RET), BF16),
        scratch_shapes=[
            pltpu.VMEM((D_C, HEADS * D_NOPE), BF16),
            pltpu.VMEM((SLOTS, D_ROPE, CMAX), BF16),
            pltpu.VMEM((D_C, HEADS * D_V), BF16),
            pltpu.VMEM((1, SLOTS), jnp.int32),
            pltpu.VMEM((SLOTS, CMAX, D_C), BF16),
            pltpu.VMEM((HEADS, SLOTS, D_C), F32),
            pltpu.VMEM((HEADS, SLOTS, 128), F32),
            pltpu.VMEM((HEADS, SLOTS, D_C), F32),
            pltpu.SemaphoreType.DMA((4,)),
            pltpu.SemaphoreType.DMA((SECTIONS,)),
        ],
        compiler_params=params(44),
        name="decode",
    )(recv, wk, cache, cache_rope, wv, pltpu.with_memory_space_constraint(order, pltpu.HBM), order.reshape(SLOTS),
      ordered_lengths.reshape(SLOTS), own[0])

    prompt_out = prefill(me, right, far, left, packed, wq, wk, wv, own, returned)
    returned = lax.all_to_all(returned, "req", 0, 0, tiled=True)

    decode_out = pl.pallas_call(
        unplace_kernel,
        out_shape=jax.ShapeDtypeStruct((ROWS, HEADS * D_V), BF16),
        compiler_params=params(16),
        name="unplace",
    )(returned, owner_row)
    return prompt_out, decode_out


def solution(mesh):
    placed = (
        P(("req", "head"), None),
        P(("req", "head"), None),
        P(None, ("req", "head")),
        P(("req", "head")),
        P(None, "head"),
        P(None, "head"),
        P(None, "head"),
        P("req", "head"),
        P("req"),
        P("req"),
        P("req", None, None),
        P("req", None, None),
        P("req"),
    )
    return jax.shard_map(
        on_device,
        mesh=mesh,
        in_specs=placed,
        out_specs=(P("req", "head"), P("req", "head")),
        check_vma=False,
    )
```

```python
import math

import jax
import jax.numpy as jnp
from jax import lax
from jax.experimental import pallas as pl
from jax.experimental.pallas import tpu as pltpu
from jax.sharding import PartitionSpec as P

D_C = 512
D_NOPE = 128
D_ROPE = 64
D_V = 128
D_Q = 1536
HEADS = 16
TOKENS = 512
CHUNK = 128
ROWS = 64
MOST = 4
SLOTS = 64
CMAX = 256
PEERS = 32
PACK = D_Q + D_C + 128
SEND = 1536 + 128
RET = 1024
ROPE_BASE = 10000.0
SCALE = (D_NOPE + D_ROPE) ** -0.5
SCALE_LOG2 = SCALE * math.log2(math.e)
MASKED = -1e30
F32 = jnp.float32
BF16 = jnp.bfloat16
MIB = 1024 * 1024


def iota(shape, dim):
    return lax.broadcasted_iota(jnp.int32, shape, dim)


def dot(a, b, dims=((1,), (0,))):
    return lax.dot_general(a, b, (dims, ((), ())), preferred_element_type=F32)


def frequencies():
    return jnp.exp(iota((32, 128), 0).astype(F32) * (-math.log(ROPE_BASE) / 32.0))[:, :1]


def column_of(row):
    n = row.shape[1]
    eye = iota((n, n), 0) == iota((n, n), 1)
    return jnp.sum(jnp.where(eye, row, 0), axis=1, keepdims=True)


def pack_kernel(x_ref, l_ref, rk_ref, pos_ref, len_ref, after_ref, packed_ref, plan_ref):
    packed_ref[:, :D_Q] = x_ref[...]
    packed_ref[:, D_Q:D_Q + D_C] = l_ref[...]
    pos = pos_ref[...]
    angle = pos.astype(F32) * frequencies()
    cos, sin = jnp.cos(angle), jnp.sin(angle)
    keys = rk_ref[...].astype(F32)
    first, second = keys[:32], keys[32:]
    high = (pos >> 4).astype(F32)
    low = (pos & 15).astype(F32)
    place = iota((64, CHUNK), 0)
    tail = jnp.where(place == 0, high, jnp.where(place == 1, low, 0.0))
    block = jnp.concatenate([first * cos - second * sin, first * sin + second * cos, tail], axis=0)
    packed_ref[:, D_Q + D_C:] = block.T.astype(BF16)

    length = len_ref[...]
    length_col = column_of(length)
    this, other = iota((SLOTS, SLOTS), 0), iota((SLOTS, SLOTS), 1)
    ahead = (length < length_col) | ((length == length_col) & (other < this))
    rank = jnp.sum(jnp.where(ahead, 1, 0), axis=1, keepdims=True)
    hit = rank == other
    plan_ref[...] = jnp.sum(
        jnp.concatenate([jnp.where(hit, this, 0), jnp.where(hit, length_col, 0)], axis=1), axis=0, keepdims=True)


def place_kernel(q_hbm, owner_hbm, slot_hbm, send_hbm, q_ref, owner_ref, slot_ref, send_ref, sems, send_sems):
    copies = [pltpu.make_async_copy(src, dst, sems.at[i]) for i, (src, dst) in enumerate(
        ((owner_hbm, owner_ref), (slot_hbm, slot_ref), (q_hbm, q_ref)))]
    for copy in copies:
        copy.start()
    for copy in copies[:2]:
        copy.wait()
    owner = owner_ref[...]
    owner_col = column_of(owner)
    same = owner_col == owner
    before = iota((ROWS, ROWS), 0) < iota((ROWS, ROWS), 1)
    rank = jnp.sum(jnp.where(same & before, 1, 0), axis=0, keepdims=True)
    target = owner * (2 * MOST) + rank
    target = jnp.concatenate([target, target + MOST], axis=1)
    placing = iota((PEERS * 2 * MOST, 2 * ROWS), 0) == target
    spread = placing.astype(BF16)
    slot = slot_ref[...] + 1
    slot = jnp.concatenate([slot, slot], axis=1)
    slot_col = jnp.sum(jnp.where(placing, slot, 0), axis=1, keepdims=True)
    parts = [(0, 512), (512, 512), (1024, SEND - 1024)]
    sends = [pltpu.make_async_copy(send_ref.at[:, pl.ds(at, width)], send_hbm.at[:, pl.ds(at, width)], send_sems.at[i])
             for i, (at, width) in enumerate(parts)]
    send_ref[:, 1536:] = jnp.broadcast_to(slot_col.astype(F32), (PEERS * 2 * MOST, 128)).astype(BF16)
    copies[2].wait()
    for part, send in enumerate(sends):
        lanes = slice(part * 512, (part + 1) * 512)
        queries = jnp.concatenate([q_ref[:, lanes], q_ref[:, 1536 + part * 512:1536 + (part + 1) * 512]], axis=0)
        send_ref[:, lanes] = dot(spread, queries).astype(BF16)
        send.start()
    for send in sends:
        send.wait()


def split_pair(three):
    low_lane = iota((three.shape[0], 128), 1) < 64
    second, third = three[:, 128:256], three[:, 256:]
    rotary = jnp.where(low_lane, second, third)
    odd = pltpu.roll(jnp.where(low_lane, third, second), 64, 1)
    return three[:, :128], odd, rotary


TOGETHER = 8
WIDE = TOGETHER * HEADS
SECTION = 16
SECTIONS = SLOTS // SECTION
WIDTHS = (64, 128, 192, 256)


def decode_kernel(recv_ref, kup_hbm, lat_hbm, rk_hbm, vup_hbm, plan_hbm, after_ref, out_hbm,
                  kup_ref, rk_ref, vup_ref, plan_row_ref, plan_ref, out_ref, lat_ref, lq_ref, qr_ref, lo_ref, sems, lat_sems, out_sem):
    rows = PEERS * 2 * MOST
    plan_copy, kup_copy, rk_copy, vup_copy, row_copy = [
        pltpu.make_async_copy(src, dst, sems.at[i]) for i, (src, dst) in enumerate(
            ((plan_hbm, plan_ref), (kup_hbm, kup_ref.at[:, pl.ds(0, HEADS * D_NOPE)]), (rk_hbm, rk_ref), (vup_hbm, vup_ref.at[:, pl.ds(0, HEADS * D_V)]), (plan_hbm, plan_row_ref)))]

    def of_width(section, width):
        longest = plan_ref[0, SLOTS + section * SECTION + SECTION - 1]
        return (longest <= width) & (longest > width - 64)

    def fetch(section, width, i):
        place = section * SECTION + i
        return pltpu.make_async_copy(
            lat_hbm.at[plan_ref[0, place], pl.ds(0, width)], lat_ref.at[place, pl.ds(0, width), pl.ds(0, D_C)], lat_sems.at[section])

    def start(section):
        for width in WIDTHS:
            @pl.when(of_width(section, width))
            def _():
                for i in range(SECTION):
                    fetch(section, width, i).start()

    plan_copy.start()
    row_copy.start()
    kup_copy.start()
    plan_copy.wait()
    start(0)
    rk_copy.start()

    def place_onehot():
        slot_col = recv_ref[:, 1536:].astype(jnp.int32)
        hit = slot_col[:, :SLOTS] == plan_row_ref[:, :SLOTS] + 1
        half = (iota((rows, SLOTS), 0) & 7) < MOST
        return hit & half, hit & jnp.logical_not(half)

    row_copy.wait()
    first, second = place_onehot()
    blank = jnp.zeros((SLOTS, 128), BF16)
    low_lane = iota((SLOTS, 128), 1) < 64
    spreads = [jnp.concatenate([jnp.where(hit, 1.0, 0.0), jnp.zeros((rows, 64), F32)], axis=1).T[:SLOTS].astype(BF16)
               for hit in (first, second)]
    queries = [dot(spread, recv_ref[:, :1536]) for spread in spreads]
    kup_copy.wait()
    start(1)
    for side in range(2):
        for pair in range(4):
            head = side * 8 + pair * 2
            even, odd, rotary = split_pair(queries[side][:, pair * 384:(pair + 1) * 384])
            both = jnp.concatenate([jnp.concatenate([even.astype(BF16), blank], axis=1),
                                    jnp.concatenate([blank, odd.astype(BF16)], axis=1)], axis=0)
            latent = dot(both, kup_ref[:, head * 128:(head + 2) * 128], ((1,), (1,)))
            lq_ref[head:head + 2] = latent.astype(BF16).astype(F32).reshape(2, SLOTS, D_C)
            turned = pltpu.roll(rotary, 64, 1)
            qr_ref[head] = jnp.where(low_lane, rotary, turned)
            qr_ref[head + 1] = jnp.where(low_lane, turned, rotary)
    rk_copy.wait()
    start(2)

    def attend(section, width):
        whole_section = pl.ds(pl.multiple_of(section * SECTION, SECTION), SECTION)
        pltpu.make_async_copy(
            lat_hbm.at[whole_section, pl.ds(0, width)], lat_ref.at[whole_section, pl.ds(0, width), pl.ds(0, D_C)],
            lat_sems.at[section]).wait()
        row, lane = iota((WIDE, WIDE), 0), iota((WIDE, WIDE), 1)
        by_place = jnp.where(lane == (row & 15) * TOGETHER + (row >> 4), 1.0, 0.0).astype(BF16)
        by_head = jnp.where(row == (lane & 15) * TOGETHER + (lane >> 4), 1.0, 0.0).astype(BF16)
        row_place = iota((WIDE, 1), 0) >> 4
        starts = [pl.multiple_of(section * SECTION + group * TOGETHER, TOGETHER) for group in range(SECTION // TOGETHER)]
        queries = []
        for start in starts:
            latent = lq_ref[:, pl.ds(start, TOGETHER), :].reshape(WIDE, D_C).astype(BF16)
            rotary = qr_ref[:, pl.ds(start, TOGETHER), :].reshape(WIDE, 128).astype(BF16)
            queries.append((dot(by_place, latent).astype(BF16), dot(by_place, rotary).astype(BF16)))
        scores = []
        for start, (latent, rotary) in zip(starts, queries):
            score = []
            length = jnp.full((WIDE, 1), plan_ref[0, SLOTS + start], jnp.int32)
            for i in range(TOGETHER):
                mine = slice(i * HEADS, (i + 1) * HEADS)
                score.append(dot(latent[mine], lat_ref[start + i, :width, :D_C], ((1,), (1,)))
                             + dot(rotary[mine, :D_ROPE], rk_ref[plan_ref[0, start + i], :, :width]))
                length = jnp.where(row_place == i, plan_ref[0, SLOTS + start + i], length)
            score = jnp.concatenate(score, axis=0)
            scores.append(jnp.where(iota((WIDE, width), 1) < length, score * SCALE, MASKED))
        for start, score in zip(starts, scores):
            raised = jnp.exp(score - jnp.max(score, axis=1, keepdims=True))
            weights = (raised * (1.0 / jnp.sum(raised, axis=1, keepdims=True))).astype(BF16)
            total = jnp.concatenate(
                [dot(weights[i * HEADS:(i + 1) * HEADS], lat_ref[start + i, :width, :D_C]).astype(BF16)
                 for i in range(TOGETHER)], axis=0)
            lo_ref[:, pl.ds(start, TOGETHER), :] = dot(by_head, total).reshape(HEADS, TOGETHER, D_C)

    @pl.loop(0, SECTIONS)
    def _(section):
        @pl.when(section == 0)
        def _():
            start(SECTIONS - 1)
            vup_copy.start()

        for width in WIDTHS:
            @pl.when(of_width(section, width))
            def _():
                attend(section, width)

    vup_copy.wait()
    first, second = place_onehot()
    spread = jnp.concatenate([jnp.where(first, 1.0, 0.0), jnp.where(second, 1.0, 0.0)], axis=1).astype(BF16)
    outs = []
    for head in range(0, HEADS, 2):
        latent_out = lo_ref[head:head + 2].reshape(2 * SLOTS, D_C).astype(BF16)
        both = dot(latent_out, vup_ref[:, head * 128:(head + 2) * 128]).astype(BF16)
        outs += [both[:SLOTS, :128], both[SLOTS:, 128:]]
    outs = jnp.concatenate([jnp.concatenate(outs[:8], axis=1), jnp.concatenate(outs[8:], axis=1)], axis=0)
    out_ref[...] = dot(spread, outs).astype(BF16)
    out_copy = pltpu.make_async_copy(out_ref, out_hbm, out_sem)
    out_copy.start()
    out_copy.wait()


def unplace_kernel(ret_ref, owner_ref, out_ref):
    owner = owner_ref[...]
    owner_col = column_of(owner)
    before = iota((ROWS, ROWS), 1) < iota((ROWS, ROWS), 0)
    rank = jnp.sum(jnp.where((owner_col == owner) & before, 1, 0), axis=1, keepdims=True)
    target = owner_col * (2 * MOST) + rank
    lane = iota((ROWS, PEERS * 2 * MOST), 1)
    for side in range(2):
        spread = jnp.where(lane == target + side * MOST, 1.0, 0.0).astype(BF16)
        out_ref[:, side * RET:(side + 1) * RET] = dot(spread, ret_ref[...]).astype(BF16)


GROUP = 4


GROUPS = HEADS // GROUP


def fetch_weights(group, sources, buffers, sems):
    return [pltpu.make_async_copy(
        src.at[:, pl.ds(pl.multiple_of(group * width, 128), width)], dst.at[group], sems.at[i, group])
        for i, (src, dst, width) in enumerate(zip(sources, buffers, (GROUP * 192, GROUP * 128, GROUP * 128)))]


def rope_tables(extra):
    turned = extra.astype(F32).T
    pos = turned[64:65] * 16.0 + turned[65:66]
    angle = pos * frequencies()
    cos, sin = jnp.cos(angle), jnp.sin(angle)
    return (jnp.concatenate([cos, cos, cos, cos], axis=0).T, jnp.concatenate([-sin, sin, -sin, sin], axis=0).T)


def rotated(rotary, cos, sin):
    lane = iota(rotary.shape, 1) & 63
    swapped = jnp.where(lane < 32, pltpu.roll(rotary, 96, 1), pltpu.roll(rotary, 32, 1))
    return (rotary * cos + swapped * sin).astype(BF16)


def own_kernel(packed_hbm, wq_hbm, wk_hbm, wv_hbm, qn_hbm, qr_hbm, k_hbm, v_hbm,
               qn_ref, qr_ref, k_ref, v_ref, x_ref, wq_ref, wk_ref, wv_ref, cos_ref, sin_ref, x_sem, sems, out_sems):
    def fetch(group):
        return fetch_weights(group, (wq_hbm, wk_hbm, wv_hbm), (wq_ref, wk_ref, wv_ref), sems)

    def send_out(group):
        return [pltpu.make_async_copy(src.at[group], dst.at[group], out_sems.at[i, group]) for i, (src, dst) in enumerate(
            ((qn_ref, qn_hbm), (qr_ref, qr_hbm), (k_ref, k_hbm), (v_ref, v_hbm)))]

    x_copy = pltpu.make_async_copy(packed_hbm, x_ref, x_sem)
    x_copy.start()
    for copy in fetch(0):
        copy.start()
    x_copy.wait()
    for group in range(1, GROUPS):
        for copy in fetch(group):
            copy.start()
    cos_ref[...], sin_ref[...] = rope_tables(x_ref[:, D_Q + D_C:])

    @pl.loop(0, GROUPS)
    def _(group):
        for copy in fetch(group):
            copy.wait()
        queries = dot(x_ref[:, :D_Q], wq_ref[group])
        for pair in range(GROUP // 2):
            even, odd, rotary = split_pair(queries[:, pair * 384:(pair + 1) * 384])
            qn_ref[group, :, pair * 256:pair * 256 + 128] = even.astype(BF16)
            qn_ref[group, :, pair * 256 + 128:pair * 256 + 256] = odd.astype(BF16)
            qr_ref[group, :, pair * 128:(pair + 1) * 128] = rotated(rotary, cos_ref[...], sin_ref[...])
        latents = x_ref[:, D_Q:D_Q + D_C]
        k_ref[group] = dot(latents, wk_ref[group]).astype(BF16)
        v_ref[group] = dot(latents, wv_ref[group]).astype(BF16)
        for copy in send_out(group):
            copy.start()

    for group in range(GROUPS):
        for copy in send_out(group):
            copy.wait()


def prefill_kernel(right_ref, far_ref, left_ref, own_hbm, wq_hbm, wk_hbm, wv_hbm,
                   own_qn_hbm, own_qr_hbm, own_k_hbm, own_v_hbm, after_ref, out_hbm,
                   own_ref, all_wq_ref, all_wk_ref, all_wv_ref, all_out_ref, chunk_sem, weight_sems, own_sems, out_sems,
                   cos_ref, sin_ref, bias_ref, pair_ref, *sets):
    me = lax.axis_index("head")
    place = [(c - me + 3) & 3 for c in range(4)]
    half = TOKENS // 2
    sets = (sets[:4], sets[4:])
    others = (right_ref, far_ref, left_ref)
    shared_copy = pltpu.make_async_copy(own_hbm.at[:, pl.ds(D_Q + D_C, 128)], own_ref, chunk_sem)

    def fetch(group):
        return fetch_weights(group, (wq_hbm, wk_hbm, wv_hbm), (all_wq_ref, all_wk_ref, all_wv_ref), weight_sems)

    def fetch_own(group, into, parity):
        return [pltpu.make_async_copy(src.at[group], dst.at[3], own_sems.at[i, parity])
                for i, (src, dst) in enumerate(zip((own_qn_hbm, own_qr_hbm, own_k_hbm, own_v_hbm), into))]

    def send_out(group):
        return pltpu.make_async_copy(
            all_out_ref.at[group], out_hbm.at[:, pl.ds(pl.multiple_of(group * GROUP * 128, 128), GROUP * 128)],
            out_sems.at[group])

    def prepare():
        extras = [ref[:, D_Q + D_C:] for ref in others] + [own_ref[...]]
        cos_ref[...], sin_ref[...] = rope_tables(jnp.concatenate(extras[:3], axis=0))
        low_lane = iota((CHUNK, 128), 1) < 64
        for slot, extra in enumerate(extras):
            extra = extra.astype(F32)
            pos = (extra[:, 64:65] * 16.0 + extra[:, 65:66]).astype(jnp.int32)
            chunk = (slot + 1 + me) & 3
            query, key = iota((CHUNK, TOKENS), 0) + chunk * CHUNK, iota((CHUNK, TOKENS), 1)
            bias_ref[chunk] = jnp.where((key <= query) & (key >= query - pos), 0.0, MASKED)
            keep = jnp.where(low_lane, extra, 0.0)
            pair_ref[0, chunk] = keep.astype(BF16)
            pair_ref[1, chunk] = pltpu.roll(keep, 64, 1).astype(BF16)

    def project_steps(into, group):
        qn_ref, qr_ref, k_ref, v_ref = into
        wq_ref, wk_ref, wv_ref = all_wq_ref.at[group], all_wk_ref.at[group], all_wv_ref.at[group]
        rows = 3 * CHUNK
        shape = (3, CHUNK, 128)
        held = []

        def query(first, width):
            x = jnp.concatenate([ref[:, :D_Q] for ref in others], axis=0)
            held.append(dot(x, wq_ref[:, first:first + width]))

        def turn(pair):
            even, odd, rotary = split_pair(jnp.concatenate(held, axis=1)[:, pair * 384:(pair + 1) * 384])
            qn_ref[:3, :, pair * 256:pair * 256 + 128] = even.astype(BF16).reshape(shape)
            qn_ref[:3, :, pair * 256 + 128:pair * 256 + 256] = odd.astype(BF16).reshape(shape)
            qr_ref[:3, :, pair * 128:(pair + 1) * 128] = rotated(rotary, cos_ref[...], sin_ref[...]).reshape(shape)

        def latent(which):
            w_ref, to_ref = ((wk_ref, k_ref), (wv_ref, v_ref))[which - 1]
            x = jnp.concatenate([ref[:, D_Q:D_Q + D_C] for ref in others], axis=0)
            to_ref[:3] = dot(x, w_ref[...]).astype(BF16).reshape(3, CHUNK, GROUP * 128)

        return query, turn, latent

    def attend_steps(source, group):
        qn_ref, qr_ref, k_ref, v_ref = source
        out_ref = all_out_ref.at[group]
        ones = jnp.ones((CHUNK, 128), BF16)
        scores = {}

        def score(head):
            lanes = slice(head * 128, (head + 1) * 128)
            pair = slice(head // 2 * 128, (head // 2 + 1) * 128)
            query = [jnp.concatenate([qn_ref[place[c], :, lanes], qr_ref[place[c], :, pair]], axis=1) for c in range(4)]
            keys = [jnp.concatenate([k_ref[place[c], :, lanes], pair_ref[head % 2, c]], axis=1) for c in range(4)]
            bias = bias_ref[...].reshape(TOKENS, TOKENS)
            early = dot(jnp.concatenate(query, axis=0), jnp.concatenate(keys[:2], axis=0), ((1,), (1,)))
            late = dot(jnp.concatenate(query[2:], axis=0), jnp.concatenate(keys[2:], axis=0), ((1,), (1,)))
            scores[head] = early + bias[:, :half], late + bias[half:, half:]

        def weigh(head):
            lanes = slice(head * 128, (head + 1) * 128)
            early, late = scores[head]
            values = [jnp.concatenate([v_ref[place[c], :, lanes], ones], axis=1) for c in range(4)]
            top = jnp.max(early[:half], axis=1, keepdims=True)
            raised = jnp.exp2((early[:half] - top) * SCALE_LOG2).astype(BF16)
            top_late = jnp.max(jnp.maximum(early[half:], late), axis=1, keepdims=True)
            raised_late = [jnp.exp2((part - top_late) * SCALE_LOG2).astype(BF16) for part in (early[half:], late)]
            total = dot(jnp.concatenate([raised, raised_late[0]], axis=0), jnp.concatenate(values[:2], axis=0))
            total_late = total[half:] + dot(raised_late[1], jnp.concatenate(values[2:], axis=0))
            out_ref[:half, lanes] = (total[:half, :128] / total[:half, 128:]).astype(BF16)
            out_ref[half:, lanes] = (total_late[:, :128] / total_late[:, 128:]).astype(BF16)

        return score, weigh

    def step_copies(copies, act):
        for copy in copies:
            act(copy)

    start, wait = (lambda copy: copy.start()), (lambda copy: copy.wait())
    shared_copy.start()
    step_copies(fetch(0), start)
    shared_copy.wait()
    prepare()
    step_copies(fetch(0), wait)
    step_copies(fetch(1), start)
    step_copies(fetch_own(0, sets[0], 0), start)
    query, turn, latent = project_steps(sets[0], 0)
    query(0, 512)
    query(512, 256)
    turn(0)
    latent(1)
    turn(1)
    latent(2)

    @pl.loop(1, GROUPS)
    def _(step):
        step_copies(fetch(step), wait)

        @pl.when(step < GROUPS - 1)
        def _():
            step_copies(fetch(step + 1), start)

        for parity in range(2):
            @pl.when((step & 1) == parity)
            def _():
                source, into = sets[1 - parity], sets[parity]
                step_copies(fetch_own(step, into, parity), start)
                step_copies(fetch_own(step - 1, source, 1 - parity), wait)
                score, weigh = attend_steps(source, step - 1)
                query, turn, latent = project_steps(into, step)
                query(0, 512)
                score(0)
                score(1)
                weigh(0)
                query(512, 256)
                turn(0)
                score(2)
                weigh(1)
                latent(1)
                turn(1)
                score(3)
                weigh(2)
                latent(2)
                weigh(3)
        send_out(step - 1).start()

    last = GROUPS - 1
    step_copies(fetch_own(last, sets[last % 2], last % 2), wait)
    score, weigh = attend_steps(sets[last % 2], last)
    score(0)
    for head in range(GROUP):
        if head + 1 < GROUP:
            score(head + 1)
        weigh(head)
    send_out(last).start()
    step_copies([send_out(group) for group in range(GROUPS)], wait)


def in_hbm(array):
    return pltpu.with_memory_space_constraint(array, pltpu.HBM)


def whole(shape):
    return pl.BlockSpec(shape, lambda *_: (0,) * len(shape))


def params(mib):
    return pltpu.CompilerParams(vmem_limit_bytes=mib * MIB)


def smem():
    return pl.BlockSpec(memory_space=pltpu.SMEM)


def anywhere():
    return pl.BlockSpec(memory_space=pl.ANY)


def vmem():
    return pl.BlockSpec(memory_space=pltpu.VMEM)


SETS = (GROUP * 128, GROUP * 64, GROUP * 128, GROUP * 128)


WEIGHTS = [pltpu.VMEM((GROUPS, D_Q, GROUP * 192), BF16), pltpu.VMEM((GROUPS, D_C, GROUP * 128), BF16),
           pltpu.VMEM((GROUPS, D_C, GROUP * 128), BF16)]


def project_own(packed, wq, wk, wv):
    return pl.pallas_call(
        own_kernel,
        in_specs=[anywhere()] * 4,
        out_specs=[anywhere()] * 4,
        out_shape=[pltpu.HBM((GROUPS, CHUNK, width), BF16) for width in SETS],
        scratch_shapes=[pltpu.VMEM((GROUPS, CHUNK, width), BF16) for width in SETS]
        + [pltpu.VMEM((CHUNK, PACK), BF16)] + WEIGHTS + [
            pltpu.VMEM((CHUNK, 128), F32),
            pltpu.VMEM((CHUNK, 128), F32),
            pltpu.SemaphoreType.DMA,
            pltpu.SemaphoreType.DMA((3, GROUPS)),
            pltpu.SemaphoreType.DMA((4, GROUPS)),
        ],
        compiler_params=params(60),
        name="own",
    )(in_hbm(packed), wq, wk, wv)


def prefill(right, far, left, packed, wq, wk, wv, own, after):
    return pl.pallas_call(
        prefill_kernel,
        in_specs=[vmem()] * 3 + [anywhere()] * 9,
        out_specs=anywhere(),
        out_shape=jax.ShapeDtypeStruct((TOKENS, HEADS * D_V), BF16),
        scratch_shapes=[pltpu.VMEM((CHUNK, 128), BF16)] + WEIGHTS + [
            pltpu.VMEM((GROUPS, TOKENS, GROUP * 128), BF16),
            pltpu.SemaphoreType.DMA,
            pltpu.SemaphoreType.DMA((3, GROUPS)),
            pltpu.SemaphoreType.DMA((4, 2)),
            pltpu.SemaphoreType.DMA((GROUPS,)),
            pltpu.VMEM((3 * CHUNK, 128), F32),
            pltpu.VMEM((3 * CHUNK, 128), F32),
            pltpu.VMEM((4, CHUNK, TOKENS), F32),
            pltpu.VMEM((2, 4, CHUNK, 128), BF16),
        ] + [pltpu.VMEM((4, CHUNK, width), BF16) for width in SETS] * 2,
        compiler_params=params(36),
        name="prefill",
    )(right, far, left, in_hbm(packed), wq, wk, wv, *own, after)


def on_device(x, latents, rotary_keys, positions, wq, wk, wv, queries, owner, slot, cache, cache_rope, lengths):
    wq, wk, wv, cache, cache_rope = (in_hbm(array) for array in (wq, wk, wv, cache, cache_rope))
    owner_row, slot_row = owner.reshape(1, ROWS), slot.reshape(1, ROWS)
    send = pl.pallas_call(
        place_kernel,
        in_specs=[anywhere()] * 3,
        out_specs=anywhere(),
        out_shape=pltpu.HBM((PEERS * 2 * MOST, SEND), BF16),
        scratch_shapes=[
            pltpu.VMEM((ROWS, HEADS * 192), BF16),
            pltpu.VMEM((1, ROWS), jnp.int32),
            pltpu.VMEM((1, ROWS), jnp.int32),
            pltpu.VMEM((PEERS * 2 * MOST, SEND), BF16),
            pltpu.SemaphoreType.DMA((3,)),
            pltpu.SemaphoreType.DMA((3,)),
        ],
        compiler_params=params(16),
        name="place",
    )(in_hbm(queries), in_hbm(owner_row), in_hbm(slot_row))
    recv = lax.all_to_all(send, "req", 0, 0, tiled=True)

    packed, plan = pl.pallas_call(
        pack_kernel,
        in_specs=[vmem()] * 5 + [anywhere()],
        out_specs=[vmem()] * 2,
        out_shape=[jax.ShapeDtypeStruct((CHUNK, PACK), BF16), jax.ShapeDtypeStruct((1, 2 * SLOTS), jnp.int32)],
        compiler_params=params(60),
        name="pack",
    )(x, latents, rotary_keys, positions.reshape(1, CHUNK), lengths.reshape(1, SLOTS), in_hbm(send))
    right = lax.ppermute(packed, "head", [(i, (i + 3) % 4) for i in range(4)])
    left = lax.ppermute(packed, "head", [(i, (i + 1) % 4) for i in range(4)])
    far = lax.ppermute(packed, "head", [(i, (i + 2) % 4) for i in range(4)])
    own = [in_hbm(part) for part in project_own(packed, wq, wk, wv)]

    returned = pl.pallas_call(
        decode_kernel,
        in_specs=[vmem()] + [anywhere()] * 6,
        out_specs=anywhere(),
        out_shape=pltpu.HBM((PEERS * 2 * MOST, RET), BF16),
        scratch_shapes=[
            pltpu.VMEM((D_C, HEADS * D_NOPE + 128), BF16),
            pltpu.VMEM((SLOTS, D_ROPE, CMAX), BF16),
            pltpu.VMEM((D_C, HEADS * D_V + 128), BF16),
            pltpu.VMEM((1, 2 * SLOTS), jnp.int32),
            pltpu.SMEM((1, 2 * SLOTS), jnp.int32),
            pltpu.VMEM((PEERS * 2 * MOST, RET), BF16),
            pltpu.VMEM((SLOTS, CMAX, D_C + 128), BF16),
            pltpu.VMEM((HEADS, SLOTS, D_C), F32),
            pltpu.VMEM((HEADS, SLOTS, 128), F32),
            pltpu.VMEM((HEADS, SLOTS, D_C), F32),
            pltpu.SemaphoreType.DMA((5,)),
            pltpu.SemaphoreType.DMA((SECTIONS,)),
            pltpu.SemaphoreType.DMA,
        ],
        compiler_params=params(44),
        name="decode",
    )(recv, wk, cache, cache_rope, wv, in_hbm(plan), own[0])

    prompt_out = prefill(right, far, left, packed, wq, wk, wv, own, in_hbm(returned))
    returned = lax.all_to_all(returned, "req", 0, 0, tiled=True)

    decode_out = pl.pallas_call(
        unplace_kernel,
        out_shape=jax.ShapeDtypeStruct((ROWS, HEADS * D_V), BF16),
        compiler_params=params(16),
        name="unplace",
    )(returned, owner_row)
    return prompt_out, decode_out


def solution(mesh):
    placed = (
        P(("req", "head"), None),
        P(("req", "head"), None),
        P(None, ("req", "head")),
        P(("req", "head")),
        P(None, "head"),
        P(None, "head"),
        P(None, "head"),
        P("req", "head"),
        P("req"),
        P("req"),
        P("req", None, None),
        P("req", None, None),
        P("req"),
    )
    return jax.shard_map(
        on_device,
        mesh=mesh,
        in_specs=placed,
        out_specs=(P("req", "head"), P("req", "head")),
        check_vma=False,
    )
```

```python
import math

import jax
import jax.numpy as jnp
from jax import lax
from jax.experimental import pallas as pl
from jax.experimental.pallas import tpu as pltpu
from jax.sharding import PartitionSpec as P

D_C = 512
D_NOPE = 128
D_ROPE = 64
D_V = 128
D_Q = 1536
HEADS = 16
TOKENS = 512
CHUNK = 128
ROWS = 64
MOST = 4
SLOTS = 64
CMAX = 256
PEERS = 32
PACK = D_Q + D_C + 128
SEND = 1536 + 128
RET = 1024
ROPE_BASE = 10000.0
SCALE = (D_NOPE + D_ROPE) ** -0.5
SCALE_LOG2 = SCALE * math.log2(math.e)
MASKED = -1e30
F32 = jnp.float32
BF16 = jnp.bfloat16
MIB = 1024 * 1024


def iota(shape, dim):
    return lax.broadcasted_iota(jnp.int32, shape, dim)


def dot(a, b, dims=((1,), (0,))):
    return lax.dot_general(a, b, (dims, ((), ())), preferred_element_type=F32)


def frequencies():
    return jnp.exp(iota((32, 128), 0).astype(F32) * (-math.log(ROPE_BASE) / 32.0))[:, :1]


def column_of(row):
    n = row.shape[1]
    eye = iota((n, n), 0) == iota((n, n), 1)
    return jnp.sum(jnp.where(eye, row, 0), axis=1, keepdims=True)


def stage_kernel(q_hbm, owner_hbm, slot_hbm, x_hbm, l_hbm, rk_hbm, pos_hbm, len_hbm, send_hbm, packed_hbm, plan_ref,
                 q_ref, owner_ref, slot_ref, packed_ref, rk_ref, pos_ref, len_ref, send_ref, sems, out_sems):
    moves = [(owner_hbm, owner_ref), (slot_hbm, slot_ref), (q_hbm, q_ref), (rk_hbm, rk_ref), (pos_hbm, pos_ref),
             (len_hbm, len_ref), (x_hbm, packed_ref.at[:, pl.ds(0, D_Q)]), (l_hbm, packed_ref.at[:, pl.ds(D_Q, D_C)])]
    copies = [pltpu.make_async_copy(src, dst, sems.at[i]) for i, (src, dst) in enumerate(moves)]
    send_out = pltpu.make_async_copy(send_ref, send_hbm, out_sems.at[0])
    packed_out = pltpu.make_async_copy(packed_ref, packed_hbm, out_sems.at[1])
    for copy in copies:
        copy.start()
    for copy in copies[:3]:
        copy.wait()
    owner = owner_ref[...]
    owner_col = column_of(owner)
    same = owner_col == owner
    before = iota((ROWS, ROWS), 0) < iota((ROWS, ROWS), 1)
    rank = jnp.sum(jnp.where(same & before, 1, 0), axis=0, keepdims=True)
    target = owner * (2 * MOST) + rank
    target = jnp.concatenate([target, target + MOST], axis=1)
    placing = iota((PEERS * 2 * MOST, 2 * ROWS), 0) == target
    queries = jnp.concatenate([q_ref[:, :1536], q_ref[:, 1536:]], axis=0)
    send_ref[:, :1536] = dot(placing.astype(BF16), queries).astype(BF16)
    slot = slot_ref[...] + 1
    slot = jnp.concatenate([slot, slot], axis=1)
    slot_col = jnp.sum(jnp.where(placing, slot, 0), axis=1, keepdims=True)
    send_ref[:, 1536:] = jnp.broadcast_to(slot_col.astype(F32), (PEERS * 2 * MOST, 128)).astype(BF16)
    send_out.start()

    for copy in copies[3:]:
        copy.wait()
    pos = pos_ref[...]
    angle = pos.astype(F32) * frequencies()
    cos, sin = jnp.cos(angle), jnp.sin(angle)
    keys = rk_ref[...].astype(F32)
    first, second = keys[:32], keys[32:]
    high = (pos >> 4).astype(F32)
    low = (pos & 15).astype(F32)
    place = iota((64, CHUNK), 0)
    tail = jnp.where(place == 0, high, jnp.where(place == 1, low, 0.0))
    block = jnp.concatenate([first * cos - second * sin, first * sin + second * cos, tail], axis=0)
    packed_ref[:, D_Q + D_C:] = block.T.astype(BF16)
    packed_out.start()

    length = len_ref[...]
    length_col = column_of(length)
    this, other = iota((SLOTS, SLOTS), 0), iota((SLOTS, SLOTS), 1)
    ahead = (length < length_col) | ((length == length_col) & (other < this))
    rank = jnp.sum(jnp.where(ahead, 1, 0), axis=1, keepdims=True)
    hit = rank == other
    plan_ref[...] = jnp.sum(
        jnp.concatenate([jnp.where(hit, this, 0), jnp.where(hit, length_col, 0)], axis=1), axis=0, keepdims=True)
    send_out.wait()
    packed_out.wait()


def split_pair(three):
    low_lane = iota((three.shape[0], 128), 1) < 64
    second, third = three[:, 128:256], three[:, 256:]
    rotary = jnp.where(low_lane, second, third)
    odd = pltpu.roll(jnp.where(low_lane, third, second), 64, 1)
    return three[:, :128], odd, rotary


TOGETHER = 8
WIDE = TOGETHER * HEADS
SECTION = 16
SECTIONS = SLOTS // SECTION
WIDTHS = (64, 128, 192, 256)


def decode_kernel(recv_ref, kup_hbm, lat_hbm, rk_hbm, vup_hbm, plan_hbm, after_ref, out_hbm,
                  kup_ref, rk_ref, vup_ref, plan_row_ref, plan_ref, out_ref, lat_ref, lq_ref, qr_ref, lo_ref, sems, lat_sems, out_sem):
    rows = PEERS * 2 * MOST
    plan_copy, kup_copy, rk_copy, vup_copy, row_copy = [
        pltpu.make_async_copy(src, dst, sems.at[i]) for i, (src, dst) in enumerate(
            ((plan_hbm, plan_ref), (kup_hbm, kup_ref.at[:, pl.ds(0, HEADS * D_NOPE)]), (rk_hbm, rk_ref), (vup_hbm, vup_ref.at[:, pl.ds(0, HEADS * D_V)]), (plan_hbm, plan_row_ref)))]

    def of_width(section, width):
        longest = plan_ref[0, SLOTS + section * SECTION + SECTION - 1]
        return (longest <= width) & (longest > width - 64)

    def fetch(section, width, i):
        place = section * SECTION + i
        return pltpu.make_async_copy(
            lat_hbm.at[plan_ref[0, place], pl.ds(0, width)], lat_ref.at[place, pl.ds(0, width), pl.ds(0, D_C)], lat_sems.at[section])

    def start(section):
        for width in WIDTHS:
            @pl.when(of_width(section, width))
            def _():
                for i in range(SECTION):
                    fetch(section, width, i).start()

    plan_copy.start()
    row_copy.start()
    kup_copy.start()
    plan_copy.wait()
    start(0)
    rk_copy.start()

    def place_onehot():
        slot_col = recv_ref[:, 1536:].astype(jnp.int32)
        hit = slot_col[:, :SLOTS] == plan_row_ref[:, :SLOTS] + 1
        half = (iota((rows, SLOTS), 0) & 7) < MOST
        return hit & half, hit & jnp.logical_not(half)

    row_copy.wait()
    first, second = place_onehot()
    blank = jnp.zeros((SLOTS, 128), BF16)
    low_lane = iota((SLOTS, 128), 1) < 64
    spreads = [jnp.concatenate([jnp.where(hit, 1.0, 0.0), jnp.zeros((rows, 64), F32)], axis=1).T[:SLOTS].astype(BF16)
               for hit in (first, second)]
    queries = [dot(spread, recv_ref[:, :1536]) for spread in spreads]
    kup_copy.wait()
    start(1)
    for side in range(2):
        for pair in range(4):
            head = side * 8 + pair * 2
            even, odd, rotary = split_pair(queries[side][:, pair * 384:(pair + 1) * 384])
            both = jnp.concatenate([jnp.concatenate([even.astype(BF16), blank], axis=1),
                                    jnp.concatenate([blank, odd.astype(BF16)], axis=1)], axis=0)
            latent = dot(both, kup_ref[:, head * 128:(head + 2) * 128], ((1,), (1,)))
            lq_ref[head:head + 2] = latent.astype(BF16).astype(F32).reshape(2, SLOTS, D_C)
            turned = pltpu.roll(rotary, 64, 1)
            qr_ref[head] = jnp.where(low_lane, rotary, turned)
            qr_ref[head + 1] = jnp.where(low_lane, turned, rotary)
    rk_copy.wait()
    start(2)

    def attend(section, width):
        whole_section = pl.ds(pl.multiple_of(section * SECTION, SECTION), SECTION)
        pltpu.make_async_copy(
            lat_hbm.at[whole_section, pl.ds(0, width)], lat_ref.at[whole_section, pl.ds(0, width), pl.ds(0, D_C)],
            lat_sems.at[section]).wait()
        row, lane = iota((WIDE, WIDE), 0), iota((WIDE, WIDE), 1)
        by_place = jnp.where(lane == (row & 15) * TOGETHER + (row >> 4), 1.0, 0.0).astype(BF16)
        by_head = jnp.where(row == (lane & 15) * TOGETHER + (lane >> 4), 1.0, 0.0).astype(BF16)
        row_place = iota((WIDE, 1), 0) >> 4
        starts = [pl.multiple_of(section * SECTION + group * TOGETHER, TOGETHER) for group in range(SECTION // TOGETHER)]
        queries = []
        for start in starts:
            latent = lq_ref[:, pl.ds(start, TOGETHER), :].reshape(WIDE, D_C).astype(BF16)
            rotary = qr_ref[:, pl.ds(start, TOGETHER), :].reshape(WIDE, 128).astype(BF16)
            queries.append((dot(by_place, latent).astype(BF16), dot(by_place, rotary).astype(BF16)))
        scores = []
        for start, (latent, rotary) in zip(starts, queries):
            score = []
            length = jnp.full((WIDE, 1), plan_ref[0, SLOTS + start], jnp.int32)
            for i in range(TOGETHER):
                mine = slice(i * HEADS, (i + 1) * HEADS)
                score.append(dot(latent[mine], lat_ref[start + i, :width, :D_C], ((1,), (1,)))
                             + dot(rotary[mine, :D_ROPE], rk_ref[plan_ref[0, start + i], :, :width]))
                length = jnp.where(row_place == i, plan_ref[0, SLOTS + start + i], length)
            score = jnp.concatenate(score, axis=0)
            scores.append(jnp.where(iota((WIDE, width), 1) < length, score * SCALE, MASKED))
        for start, score in zip(starts, scores):
            raised = jnp.exp(score - jnp.max(score, axis=1, keepdims=True))
            weights = (raised * (1.0 / jnp.sum(raised, axis=1, keepdims=True))).astype(BF16)
            total = jnp.concatenate(
                [dot(weights[i * HEADS:(i + 1) * HEADS], lat_ref[start + i, :width, :D_C]).astype(BF16)
                 for i in range(TOGETHER)], axis=0)
            lo_ref[:, pl.ds(start, TOGETHER), :] = dot(by_head, total).reshape(HEADS, TOGETHER, D_C)

    @pl.loop(0, SECTIONS)
    def _(section):
        @pl.when(section == 0)
        def _():
            start(SECTIONS - 1)
            vup_copy.start()

        for width in WIDTHS:
            @pl.when(of_width(section, width))
            def _():
                attend(section, width)

    vup_copy.wait()
    first, second = place_onehot()
    spread = jnp.concatenate([jnp.where(first, 1.0, 0.0), jnp.where(second, 1.0, 0.0)], axis=1).astype(BF16)
    outs = []
    for head in range(0, HEADS, 2):
        latent_out = lo_ref[head:head + 2].reshape(2 * SLOTS, D_C).astype(BF16)
        both = dot(latent_out, vup_ref[:, head * 128:(head + 2) * 128]).astype(BF16)
        outs += [both[:SLOTS, :128], both[SLOTS:, 128:]]
    outs = jnp.concatenate([jnp.concatenate(outs[:8], axis=1), jnp.concatenate(outs[8:], axis=1)], axis=0)
    out_ref[...] = dot(spread, outs).astype(BF16)
    out_copy = pltpu.make_async_copy(out_ref, out_hbm, out_sem)
    out_copy.start()
    out_copy.wait()


def unplace_kernel(ret_ref, owner_ref, out_ref):
    owner = owner_ref[...]
    owner_col = column_of(owner)
    before = iota((ROWS, ROWS), 1) < iota((ROWS, ROWS), 0)
    rank = jnp.sum(jnp.where((owner_col == owner) & before, 1, 0), axis=1, keepdims=True)
    target = owner_col * (2 * MOST) + rank
    lane = iota((ROWS, PEERS * 2 * MOST), 1)
    for side in range(2):
        spread = jnp.where(lane == target + side * MOST, 1.0, 0.0).astype(BF16)
        out_ref[:, side * RET:(side + 1) * RET] = dot(spread, ret_ref[...]).astype(BF16)


GROUP = 4


GROUPS = HEADS // GROUP


def fetch_weights(group, sources, buffers, sems):
    return [pltpu.make_async_copy(
        src.at[:, pl.ds(pl.multiple_of(group * width, 128), width)], dst.at[group], sems.at[i, group])
        for i, (src, dst, width) in enumerate(zip(sources, buffers, (GROUP * 192, GROUP * 128, GROUP * 128)))]


def rope_tables(extra):
    turned = extra.astype(F32).T
    pos = turned[64:65] * 16.0 + turned[65:66]
    angle = pos * frequencies()
    cos, sin = jnp.cos(angle), jnp.sin(angle)
    return (jnp.concatenate([cos, cos, cos, cos], axis=0).T, jnp.concatenate([-sin, sin, -sin, sin], axis=0).T)


def rotated(rotary, cos, sin):
    lane = iota(rotary.shape, 1) & 63
    swapped = jnp.where(lane < 32, pltpu.roll(rotary, 96, 1), pltpu.roll(rotary, 32, 1))
    return (rotary * cos + swapped * sin).astype(BF16)


def own_kernel(packed_hbm, wq_hbm, wk_hbm, wv_hbm, qn_hbm, qr_hbm, k_hbm, v_hbm,
               qn_ref, qr_ref, k_ref, v_ref, x_ref, wq_ref, wk_ref, wv_ref, cos_ref, sin_ref, x_sem, sems, out_sems):
    def fetch(group):
        return fetch_weights(group, (wq_hbm, wk_hbm, wv_hbm), (wq_ref, wk_ref, wv_ref), sems)

    def send_out(group):
        return [pltpu.make_async_copy(src.at[group], dst.at[group], out_sems.at[i, group]) for i, (src, dst) in enumerate(
            ((qn_ref, qn_hbm), (qr_ref, qr_hbm), (k_ref, k_hbm), (v_ref, v_hbm)))]

    x_copy = pltpu.make_async_copy(packed_hbm, x_ref, x_sem)
    x_copy.start()
    for copy in fetch(0):
        copy.start()
    x_copy.wait()
    for group in range(1, GROUPS):
        for copy in fetch(group):
            copy.start()
    cos_ref[...], sin_ref[...] = rope_tables(x_ref[:, D_Q + D_C:])

    @pl.loop(0, GROUPS)
    def _(group):
        for_queries, for_keys, for_values = fetch(group)
        for_queries.wait()
        queries = dot(x_ref[:, :D_Q], wq_ref[group])
        for pair in range(GROUP // 2):
            even, odd, rotary = split_pair(queries[:, pair * 384:(pair + 1) * 384])
            qn_ref[group, :, pair * 256:pair * 256 + 128] = even.astype(BF16)
            qn_ref[group, :, pair * 256 + 128:pair * 256 + 256] = odd.astype(BF16)
            qr_ref[group, :, pair * 128:(pair + 1) * 128] = rotated(rotary, cos_ref[...], sin_ref[...])
        for_keys.wait()
        for_values.wait()
        latents = x_ref[:, D_Q:D_Q + D_C]
        k_ref[group] = dot(latents, wk_ref[group]).astype(BF16)
        v_ref[group] = dot(latents, wv_ref[group]).astype(BF16)
        for copy in send_out(group):
            copy.start()

    for group in range(GROUPS):
        for copy in send_out(group):
            copy.wait()


def prefill_kernel(right_ref, far_ref, left_ref, own_hbm, wq_hbm, wk_hbm, wv_hbm,
                   own_qn_hbm, own_qr_hbm, own_k_hbm, own_v_hbm, after_ref, out_hbm,
                   own_ref, all_wq_ref, all_wk_ref, all_wv_ref, all_out_ref, chunk_sem, weight_sems, own_sems, out_sems,
                   cos_ref, sin_ref, bias_ref, pair_ref, *sets):
    me = lax.axis_index("head")
    place = [(c - me + 3) & 3 for c in range(4)]
    half = TOKENS // 2
    sets = (sets[:4], sets[4:])
    others = (right_ref, far_ref, left_ref)
    shared_copy = pltpu.make_async_copy(own_hbm.at[:, pl.ds(D_Q + D_C, 128)], own_ref, chunk_sem)

    def fetch(group):
        return fetch_weights(group, (wq_hbm, wk_hbm, wv_hbm), (all_wq_ref, all_wk_ref, all_wv_ref), weight_sems)

    def fetch_own(group, into, parity):
        return [pltpu.make_async_copy(src.at[group], dst.at[3], own_sems.at[i, parity])
                for i, (src, dst) in enumerate(zip((own_qn_hbm, own_qr_hbm, own_k_hbm, own_v_hbm), into))]

    def send_out(group):
        return pltpu.make_async_copy(
            all_out_ref.at[group], out_hbm.at[:, pl.ds(pl.multiple_of(group * GROUP * 128, 128), GROUP * 128)],
            out_sems.at[group])

    def prepare():
        extras = [ref[:, D_Q + D_C:] for ref in others] + [own_ref[...]]
        cos_ref[...], sin_ref[...] = rope_tables(jnp.concatenate(extras[:3], axis=0))
        low_lane = iota((CHUNK, 128), 1) < 64
        for slot, extra in enumerate(extras):
            extra = extra.astype(F32)
            pos = (extra[:, 64:65] * 16.0 + extra[:, 65:66]).astype(jnp.int32)
            chunk = (slot + 1 + me) & 3
            query, key = iota((CHUNK, TOKENS), 0) + chunk * CHUNK, iota((CHUNK, TOKENS), 1)
            bias_ref[chunk] = jnp.where((key <= query) & (key >= query - pos), 0.0, MASKED)
            keep = jnp.where(low_lane, extra, 0.0)
            pair_ref[0, chunk] = keep.astype(BF16)
            pair_ref[1, chunk] = pltpu.roll(keep, 64, 1).astype(BF16)

    def project_steps(into, group):
        qn_ref, qr_ref, k_ref, v_ref = into
        wq_ref, wk_ref, wv_ref = all_wq_ref.at[group], all_wk_ref.at[group], all_wv_ref.at[group]
        rows = 3 * CHUNK
        shape = (3, CHUNK, 128)
        held = []

        def query(first, width):
            x = jnp.concatenate([ref[:, :D_Q] for ref in others], axis=0)
            held.append(dot(x, wq_ref[:, first:first + width]))

        def turn(pair):
            even, odd, rotary = split_pair(jnp.concatenate(held, axis=1)[:, pair * 384:(pair + 1) * 384])
            qn_ref[:3, :, pair * 256:pair * 256 + 128] = even.astype(BF16).reshape(shape)
            qn_ref[:3, :, pair * 256 + 128:pair * 256 + 256] = odd.astype(BF16).reshape(shape)
            qr_ref[:3, :, pair * 128:(pair + 1) * 128] = rotated(rotary, cos_ref[...], sin_ref[...]).reshape(shape)

        def latent(which):
            w_ref, to_ref = ((wk_ref, k_ref), (wv_ref, v_ref))[which - 1]
            x = jnp.concatenate([ref[:, D_Q:D_Q + D_C] for ref in others], axis=0)
            to_ref[:3] = dot(x, w_ref[...]).astype(BF16).reshape(3, CHUNK, GROUP * 128)

        return query, turn, latent

    def attend_steps(source, group):
        qn_ref, qr_ref, k_ref, v_ref = source
        out_ref = all_out_ref.at[group]
        ones = jnp.ones((CHUNK, 128), BF16)
        scores = {}

        def score(head):
            lanes = slice(head * 128, (head + 1) * 128)
            pair = slice(head // 2 * 128, (head // 2 + 1) * 128)
            query = [jnp.concatenate([qn_ref[place[c], :, lanes], qr_ref[place[c], :, pair]], axis=1) for c in range(4)]
            keys = [jnp.concatenate([k_ref[place[c], :, lanes], pair_ref[head % 2, c]], axis=1) for c in range(4)]
            bias = bias_ref[...].reshape(TOKENS, TOKENS)
            early = dot(jnp.concatenate(query, axis=0), jnp.concatenate(keys[:2], axis=0), ((1,), (1,)))
            late = dot(jnp.concatenate(query[2:], axis=0), jnp.concatenate(keys[2:], axis=0), ((1,), (1,)))
            scores[head] = early + bias[:, :half], late + bias[half:, half:]

        def weigh(head):
            lanes = slice(head * 128, (head + 1) * 128)
            early, late = scores[head]
            values = [jnp.concatenate([v_ref[place[c], :, lanes], ones], axis=1) for c in range(4)]
            top = jnp.max(early[:half], axis=1, keepdims=True)
            raised = jnp.exp2((early[:half] - top) * SCALE_LOG2).astype(BF16)
            top_late = jnp.max(jnp.maximum(early[half:], late), axis=1, keepdims=True)
            raised_late = [jnp.exp2((part - top_late) * SCALE_LOG2).astype(BF16) for part in (early[half:], late)]
            total = dot(jnp.concatenate([raised, raised_late[0]], axis=0), jnp.concatenate(values[:2], axis=0))
            total_late = total[half:] + dot(raised_late[1], jnp.concatenate(values[2:], axis=0))
            out_ref[:half, lanes] = (total[:half, :128] / total[:half, 128:]).astype(BF16)
            out_ref[half:, lanes] = (total_late[:, :128] / total_late[:, 128:]).astype(BF16)

        return score, weigh

    def step_copies(copies, act):
        for copy in copies:
            act(copy)

    start, wait = (lambda copy: copy.start()), (lambda copy: copy.wait())
    shared_copy.start()
    step_copies(fetch(0), start)
    shared_copy.wait()
    prepare()
    step_copies(fetch(0), wait)
    step_copies(fetch(1), start)
    step_copies(fetch_own(0, sets[0], 0), start)
    query, turn, latent = project_steps(sets[0], 0)
    query(0, 512)
    query(512, 256)
    turn(0)
    latent(1)
    turn(1)
    latent(2)

    @pl.loop(1, GROUPS)
    def _(step):
        step_copies(fetch(step), wait)

        @pl.when(step < GROUPS - 1)
        def _():
            step_copies(fetch(step + 1), start)

        for parity in range(2):
            @pl.when((step & 1) == parity)
            def _():
                source, into = sets[1 - parity], sets[parity]
                step_copies(fetch_own(step, into, parity), start)
                step_copies(fetch_own(step - 1, source, 1 - parity), wait)
                score, weigh = attend_steps(source, step - 1)
                query, turn, latent = project_steps(into, step)
                query(0, 512)
                score(0)
                score(1)
                weigh(0)
                query(512, 256)
                turn(0)
                score(2)
                weigh(1)
                latent(1)
                turn(1)
                score(3)
                weigh(2)
                latent(2)
                weigh(3)
        send_out(step - 1).start()

    last = GROUPS - 1
    step_copies(fetch_own(last, sets[last % 2], last % 2), wait)
    score, weigh = attend_steps(sets[last % 2], last)
    score(0)
    for head in range(GROUP):
        if head + 1 < GROUP:
            score(head + 1)
        weigh(head)
    send_out(last).start()
    step_copies([send_out(group) for group in range(GROUPS)], wait)


def in_hbm(array):
    return pltpu.with_memory_space_constraint(array, pltpu.HBM)


def whole(shape):
    return pl.BlockSpec(shape, lambda *_: (0,) * len(shape))


def params(mib):
    return pltpu.CompilerParams(vmem_limit_bytes=mib * MIB)


def smem():
    return pl.BlockSpec(memory_space=pltpu.SMEM)


def anywhere():
    return pl.BlockSpec(memory_space=pl.ANY)


def vmem():
    return pl.BlockSpec(memory_space=pltpu.VMEM)


SETS = (GROUP * 128, GROUP * 64, GROUP * 128, GROUP * 128)


WEIGHTS = [pltpu.VMEM((GROUPS, D_Q, GROUP * 192), BF16), pltpu.VMEM((GROUPS, D_C, GROUP * 128), BF16),
           pltpu.VMEM((GROUPS, D_C, GROUP * 128), BF16)]


def project_own(packed, wq, wk, wv):
    return pl.pallas_call(
        own_kernel,
        in_specs=[anywhere()] * 4,
        out_specs=[anywhere()] * 4,
        out_shape=[pltpu.HBM((GROUPS, CHUNK, width), BF16) for width in SETS],
        scratch_shapes=[pltpu.VMEM((GROUPS, CHUNK, width), BF16) for width in SETS]
        + [pltpu.VMEM((CHUNK, PACK), BF16)] + WEIGHTS + [
            pltpu.VMEM((CHUNK, 128), F32),
            pltpu.VMEM((CHUNK, 128), F32),
            pltpu.SemaphoreType.DMA,
            pltpu.SemaphoreType.DMA((3, GROUPS)),
            pltpu.SemaphoreType.DMA((4, GROUPS)),
        ],
        compiler_params=params(60),
        name="own",
    )(in_hbm(packed), wq, wk, wv)


def prefill(right, far, left, packed, wq, wk, wv, own, after):
    return pl.pallas_call(
        prefill_kernel,
        in_specs=[vmem()] * 3 + [anywhere()] * 9,
        out_specs=anywhere(),
        out_shape=jax.ShapeDtypeStruct((TOKENS, HEADS * D_V), BF16),
        scratch_shapes=[pltpu.VMEM((CHUNK, 128), BF16)] + WEIGHTS + [
            pltpu.VMEM((GROUPS, TOKENS, GROUP * 128), BF16),
            pltpu.SemaphoreType.DMA,
            pltpu.SemaphoreType.DMA((3, GROUPS)),
            pltpu.SemaphoreType.DMA((4, 2)),
            pltpu.SemaphoreType.DMA((GROUPS,)),
            pltpu.VMEM((3 * CHUNK, 128), F32),
            pltpu.VMEM((3 * CHUNK, 128), F32),
            pltpu.VMEM((4, CHUNK, TOKENS), F32),
            pltpu.VMEM((2, 4, CHUNK, 128), BF16),
        ] + [pltpu.VMEM((4, CHUNK, width), BF16) for width in SETS] * 2,
        compiler_params=params(36),
        name="prefill",
    )(right, far, left, in_hbm(packed), wq, wk, wv, *own, after)


def on_device(x, latents, rotary_keys, positions, wq, wk, wv, queries, owner, slot, cache, cache_rope, lengths):
    wq, wk, wv, cache, cache_rope = (in_hbm(array) for array in (wq, wk, wv, cache, cache_rope))
    owner_row, slot_row = owner.reshape(1, ROWS), slot.reshape(1, ROWS)
    send, packed, plan = pl.pallas_call(
        stage_kernel,
        in_specs=[anywhere()] * 8,
        out_specs=[anywhere(), anywhere(), vmem()],
        out_shape=[pltpu.HBM((PEERS * 2 * MOST, SEND), BF16), pltpu.HBM((CHUNK, PACK), BF16),
                   jax.ShapeDtypeStruct((1, 2 * SLOTS), jnp.int32)],
        scratch_shapes=[
            pltpu.VMEM((ROWS, HEADS * 192), BF16),
            pltpu.VMEM((1, ROWS), jnp.int32),
            pltpu.VMEM((1, ROWS), jnp.int32),
            pltpu.VMEM((CHUNK, PACK), BF16),
            pltpu.VMEM((64, CHUNK), BF16),
            pltpu.VMEM((1, CHUNK), jnp.int32),
            pltpu.VMEM((1, SLOTS), jnp.int32),
            pltpu.VMEM((PEERS * 2 * MOST, SEND), BF16),
            pltpu.SemaphoreType.DMA((8,)),
            pltpu.SemaphoreType.DMA((2,)),
        ],
        compiler_params=params(60),
        name="stage",
    )(*(in_hbm(array) for array in (
        queries, owner_row, slot_row, x, latents, rotary_keys, positions.reshape(1, CHUNK), lengths.reshape(1, SLOTS))))
    recv = lax.all_to_all(send, "req", 0, 0, tiled=True)
    right = lax.ppermute(packed, "head", [(i, (i + 3) % 4) for i in range(4)])
    left = lax.ppermute(packed, "head", [(i, (i + 1) % 4) for i in range(4)])
    far = lax.ppermute(packed, "head", [(i, (i + 2) % 4) for i in range(4)])
    own = [in_hbm(part) for part in project_own(packed, wq, wk, wv)]

    returned = pl.pallas_call(
        decode_kernel,
        in_specs=[vmem()] + [anywhere()] * 6,
        out_specs=anywhere(),
        out_shape=pltpu.HBM((PEERS * 2 * MOST, RET), BF16),
        scratch_shapes=[
            pltpu.VMEM((D_C, HEADS * D_NOPE + 128), BF16),
            pltpu.VMEM((SLOTS, D_ROPE, CMAX), BF16),
            pltpu.VMEM((D_C, HEADS * D_V + 128), BF16),
            pltpu.VMEM((1, 2 * SLOTS), jnp.int32),
            pltpu.SMEM((1, 2 * SLOTS), jnp.int32),
            pltpu.VMEM((PEERS * 2 * MOST, RET), BF16),
            pltpu.VMEM((SLOTS, CMAX, D_C + 128), BF16),
            pltpu.VMEM((HEADS, SLOTS, D_C), F32),
            pltpu.VMEM((HEADS, SLOTS, 128), F32),
            pltpu.VMEM((HEADS, SLOTS, D_C), F32),
            pltpu.SemaphoreType.DMA((5,)),
            pltpu.SemaphoreType.DMA((SECTIONS,)),
            pltpu.SemaphoreType.DMA,
        ],
        compiler_params=params(44),
        name="decode",
    )(recv, wk, cache, cache_rope, wv, in_hbm(plan), own[0])

    prompt_out = prefill(right, far, left, packed, wq, wk, wv, own, in_hbm(returned))
    returned = lax.all_to_all(returned, "req", 0, 0, tiled=True)

    decode_out = pl.pallas_call(
        unplace_kernel,
        out_shape=jax.ShapeDtypeStruct((ROWS, HEADS * D_V), BF16),
        compiler_params=params(16),
        name="unplace",
    )(returned, owner_row)
    return prompt_out, decode_out


def solution(mesh):
    placed = (
        P(("req", "head"), None),
        P(("req", "head"), None),
        P(None, ("req", "head")),
        P(("req", "head")),
        P(None, "head"),
        P(None, "head"),
        P(None, "head"),
        P("req", "head"),
        P("req"),
        P("req"),
        P("req", None, None),
        P("req", None, None),
        P("req"),
    )
    return jax.shard_map(
        on_device,
        mesh=mesh,
        in_specs=placed,
        out_specs=(P("req", "head"), P("req", "head")),
        check_vma=False,
    )
```

```python
import math

import jax
import jax.numpy as jnp
from jax import lax
from jax.experimental import pallas as pl
from jax.experimental.pallas import tpu as pltpu
from jax.sharding import PartitionSpec as P

D_C = 512
D_NOPE = 128
D_ROPE = 64
D_V = 128
D_Q = 1536
HEADS = 16
TOKENS = 512
CHUNK = 128
ROWS = 64
MOST = 4
SLOTS = 64
CMAX = 256
PEERS = 32
PACK = D_Q + D_C + 128
SEND = 1536 + 128
RET = 1024
ROPE_BASE = 10000.0
SCALE = (D_NOPE + D_ROPE) ** -0.5
SCALE_LOG2 = SCALE * math.log2(math.e)
MASKED = -1e30
F32 = jnp.float32
BF16 = jnp.bfloat16
MIB = 1024 * 1024


def iota(shape, dim):
    return lax.broadcasted_iota(jnp.int32, shape, dim)


def dot(a, b, dims=((1,), (0,))):
    return lax.dot_general(a, b, (dims, ((), ())), preferred_element_type=F32)


def frequencies():
    return jnp.exp(iota((32, 128), 0).astype(F32) * (-math.log(ROPE_BASE) / 32.0))[:, :1]


def column_of(row):
    n = row.shape[1]
    eye = iota((n, n), 0) == iota((n, n), 1)
    return jnp.sum(jnp.where(eye, row, 0), axis=1, keepdims=True)


def stage_kernel(q_hbm, owner_hbm, slot_hbm, x_hbm, l_hbm, rk_hbm, pos_hbm, len_hbm, send_hbm, packed_hbm, plan_ref,
                 q_ref, owner_ref, slot_ref, packed_ref, rk_ref, pos_ref, len_ref, send_ref, sems, out_sems):
    moves = [(owner_hbm, owner_ref), (slot_hbm, slot_ref), (pos_hbm, pos_ref), (rk_hbm, rk_ref), (q_hbm, q_ref),
             (x_hbm, packed_ref.at[:, pl.ds(0, D_Q)]), (l_hbm, packed_ref.at[:, pl.ds(D_Q, D_C)]), (len_hbm, len_ref)]
    copies = [pltpu.make_async_copy(src, dst, sems.at[i]) for i, (src, dst) in enumerate(moves)]
    send_out = pltpu.make_async_copy(send_ref, send_hbm, out_sems.at[0])
    packed_out = pltpu.make_async_copy(packed_ref, packed_hbm, out_sems.at[1])
    for copy in copies:
        copy.start()
    for copy in copies[:4]:
        copy.wait()
    owner = owner_ref[...]
    owner_col = column_of(owner)
    same = owner_col == owner
    before = iota((ROWS, ROWS), 0) < iota((ROWS, ROWS), 1)
    rank = jnp.sum(jnp.where(same & before, 1, 0), axis=0, keepdims=True)
    target = owner * (2 * MOST) + rank
    target = jnp.concatenate([target, target + MOST], axis=1)
    placing = iota((PEERS * 2 * MOST, 2 * ROWS), 0) == target
    slot = slot_ref[...] + 1
    slot = jnp.concatenate([slot, slot], axis=1)
    slot_col = jnp.sum(jnp.where(placing, slot, 0), axis=1, keepdims=True)
    send_ref[:, 1536:] = jnp.broadcast_to(slot_col.astype(F32), (PEERS * 2 * MOST, 128)).astype(BF16)
    pos = pos_ref[...]
    angle = pos.astype(F32) * frequencies()
    cos, sin = jnp.cos(angle), jnp.sin(angle)
    keys = rk_ref[...].astype(F32)
    first, second = keys[:32], keys[32:]
    high = (pos >> 4).astype(F32)
    low = (pos & 15).astype(F32)
    place = iota((64, CHUNK), 0)
    tail = jnp.where(place == 0, high, jnp.where(place == 1, low, 0.0))
    block = jnp.concatenate([first * cos - second * sin, first * sin + second * cos, tail], axis=0)
    packed_ref[:, D_Q + D_C:] = block.T.astype(BF16)
    copies[4].wait()
    queries = jnp.concatenate([q_ref[:, :1536], q_ref[:, 1536:]], axis=0)
    send_ref[:, :1536] = dot(placing.astype(BF16), queries).astype(BF16)
    send_out.start()
    for copy in copies[5:]:
        copy.wait()
    packed_out.start()

    length = len_ref[...]
    length_col = column_of(length)
    this, other = iota((SLOTS, SLOTS), 0), iota((SLOTS, SLOTS), 1)
    ahead = (length < length_col) | ((length == length_col) & (other < this))
    rank = jnp.sum(jnp.where(ahead, 1, 0), axis=1, keepdims=True)
    hit = rank == other
    plan_ref[...] = jnp.sum(
        jnp.concatenate([jnp.where(hit, this, 0), jnp.where(hit, length_col, 0)], axis=1), axis=0, keepdims=True)
    send_out.wait()
    packed_out.wait()


def split_pair(three):
    low_lane = iota((three.shape[0], 128), 1) < 64
    second, third = three[:, 128:256], three[:, 256:]
    rotary = jnp.where(low_lane, second, third)
    odd = pltpu.roll(jnp.where(low_lane, third, second), 64, 1)
    return three[:, :128], odd, rotary


TOGETHER = 8
WIDE = TOGETHER * HEADS
SECTION = 16
SECTIONS = SLOTS // SECTION
WIDTHS = ((64, 64), (64, 128), (128, 128), (128, 192), (192, 192), (192, 256), (256, 256))


def decode_kernel(recv_ref, kup_hbm, lat_hbm, rk_hbm, vup_hbm, plan_hbm, after_ref, out_hbm,
                  kup_ref, rk_ref, vup_ref, plan_row_ref, plan_ref, out_ref, lat_ref, lq_ref, qr_ref, lo_ref, sems, lat_sems, out_sem):
    rows = PEERS * 2 * MOST
    plan_copy, rk_copy, vup_copy, row_copy = [
        pltpu.make_async_copy(src, dst, sems.at[i]) for i, (src, dst) in enumerate(
            ((plan_hbm, plan_ref), (rk_hbm, rk_ref), (vup_hbm, vup_ref.at[:, pl.ds(0, HEADS * D_V)]), (plan_hbm, plan_row_ref)))]
    kup_copies = [pltpu.make_async_copy(kup_hbm.at[:, pl.ds(side * 1024, 1024)], kup_ref.at[:, pl.ds(side * 1024, 1024)],
                                        sems.at[4 + side]) for side in range(2)]

    def of_widths(section, widths):
        first, last = widths
        at = SLOTS + section * SECTION
        longest = plan_ref[0, at + SECTION - 1]
        fits = (longest <= last) & (longest > last - 64)
        if last > 64:
            short = plan_ref[0, at + TOGETHER - 1] <= last - 64
            fits = fits & (short if first < last else jnp.logical_not(short))
        return fits

    def fetch(section, widths, i):
        place = section * SECTION + i
        rows = pl.ds(0, widths[i // TOGETHER])
        return pltpu.make_async_copy(
            lat_hbm.at[plan_ref[0, place], rows], lat_ref.at[place, rows, pl.ds(0, D_C)],
            lat_sems.at[section, i // TOGETHER])

    def start(section):
        for widths in WIDTHS:
            @pl.when(of_widths(section, widths))
            def _():
                for i in range(SECTION):
                    fetch(section, widths, i).start()

    plan_copy.start()
    row_copy.start()
    for copy in kup_copies:
        copy.start()
    plan_copy.wait()
    start(0)
    rk_copy.start()

    def place_onehot():
        slot_col = recv_ref[:, 1536:].astype(jnp.int32)
        hit = slot_col[:, :SLOTS] == plan_row_ref[:, :SLOTS] + 1
        half = (iota((rows, SLOTS), 0) & 7) < MOST
        return hit & half, hit & jnp.logical_not(half)

    row_copy.wait()
    first, second = place_onehot()
    blank = jnp.zeros((SLOTS, 128), BF16)
    low_lane = iota((SLOTS, 128), 1) < 64
    spreads = [jnp.concatenate([jnp.where(hit, 1.0, 0.0), jnp.zeros((rows, 64), F32)], axis=1).T[:SLOTS].astype(BF16)
               for hit in (first, second)]
    queries = [dot(spread, recv_ref[:, :1536]) for spread in spreads]
    for side in range(2):
        kup_copies[side].wait()
        for pair in range(4):
            head = side * 8 + pair * 2
            even, odd, rotary = split_pair(queries[side][:, pair * 384:(pair + 1) * 384])
            both = jnp.concatenate([jnp.concatenate([even.astype(BF16), blank], axis=1),
                                    jnp.concatenate([blank, odd.astype(BF16)], axis=1)], axis=0)
            latent = dot(both, kup_ref[:, head * 128:(head + 2) * 128], ((1,), (1,)))
            lq_ref[head:head + 2] = latent.astype(BF16).astype(F32).reshape(2, SLOTS, D_C)
            turned = pltpu.roll(rotary, 64, 1)
            qr_ref[head] = jnp.where(low_lane, rotary, turned)
            qr_ref[head + 1] = jnp.where(low_lane, turned, rotary)
    start(1)
    rk_copy.wait()
    start(2)

    def attend(section, widths):
        for group, width in enumerate(widths):
            places = pl.ds(pl.multiple_of(section * SECTION + group * TOGETHER, TOGETHER), TOGETHER)
            pltpu.make_async_copy(
                lat_hbm.at[places, pl.ds(0, width)], lat_ref.at[places, pl.ds(0, width), pl.ds(0, D_C)],
                lat_sems.at[section, group]).wait()

        row, lane = iota((WIDE, WIDE), 0), iota((WIDE, WIDE), 1)
        by_place = jnp.where(lane == (row & 15) * TOGETHER + (row >> 4), 1.0, 0.0).astype(BF16)
        by_head = jnp.where(row == (lane & 15) * TOGETHER + (lane >> 4), 1.0, 0.0).astype(BF16)
        row_place = iota((WIDE, 1), 0) >> 4
        starts = [pl.multiple_of(section * SECTION + group * TOGETHER, TOGETHER) for group in range(SECTION // TOGETHER)]
        queries = []
        for start in starts:
            latent = lq_ref[:, pl.ds(start, TOGETHER), :].reshape(WIDE, D_C).astype(BF16)
            rotary = qr_ref[:, pl.ds(start, TOGETHER), :].reshape(WIDE, 128).astype(BF16)
            queries.append((dot(by_place, latent).astype(BF16), dot(by_place, rotary).astype(BF16)))
        scores = []
        for start, width, (latent, rotary) in zip(starts, widths, queries):
            score = []
            length = jnp.full((WIDE, 1), plan_ref[0, SLOTS + start], jnp.int32)
            for i in range(TOGETHER):
                mine = slice(i * HEADS, (i + 1) * HEADS)
                score.append(dot(latent[mine], lat_ref[start + i, :width, :D_C], ((1,), (1,)))
                             + dot(rotary[mine, :D_ROPE], rk_ref[plan_ref[0, start + i], :, :width]))
                length = jnp.where(row_place == i, plan_ref[0, SLOTS + start + i], length)
            score = jnp.concatenate(score, axis=0)
            scores.append(jnp.where(iota((WIDE, width), 1) < length, score * SCALE, MASKED))
        for start, width, score in zip(starts, widths, scores):
            raised = jnp.exp(score - jnp.max(score, axis=1, keepdims=True))
            weights = (raised * (1.0 / jnp.sum(raised, axis=1, keepdims=True))).astype(BF16)
            total = jnp.concatenate(
                [dot(weights[i * HEADS:(i + 1) * HEADS], lat_ref[start + i, :width, :D_C]).astype(BF16)
                 for i in range(TOGETHER)], axis=0)
            lo_ref[:, pl.ds(start, TOGETHER), :] = dot(by_head, total).reshape(HEADS, TOGETHER, D_C)

    @pl.loop(0, SECTIONS)
    def _(section):
        @pl.when(section == 0)
        def _():
            start(SECTIONS - 1)
            vup_copy.start()

        for widths in WIDTHS:
            @pl.when(of_widths(section, widths))
            def _():
                attend(section, widths)

    vup_copy.wait()
    first, second = place_onehot()
    spread = jnp.concatenate([jnp.where(first, 1.0, 0.0), jnp.where(second, 1.0, 0.0)], axis=1).astype(BF16)
    outs = []
    for head in range(0, HEADS, 2):
        latent_out = lo_ref[head:head + 2].reshape(2 * SLOTS, D_C).astype(BF16)
        both = dot(latent_out, vup_ref[:, head * 128:(head + 2) * 128]).astype(BF16)
        outs += [both[:SLOTS, :128], both[SLOTS:, 128:]]
    outs = jnp.concatenate([jnp.concatenate(outs[:8], axis=1), jnp.concatenate(outs[8:], axis=1)], axis=0)
    out_ref[...] = dot(spread, outs).astype(BF16)
    out_copy = pltpu.make_async_copy(out_ref, out_hbm, out_sem)
    out_copy.start()
    out_copy.wait()


def unplace_kernel(ret_ref, owner_ref, out_ref):
    owner = owner_ref[...]
    owner_col = column_of(owner)
    before = iota((ROWS, ROWS), 1) < iota((ROWS, ROWS), 0)
    rank = jnp.sum(jnp.where((owner_col == owner) & before, 1, 0), axis=1, keepdims=True)
    target = owner_col * (2 * MOST) + rank
    lane = iota((ROWS, PEERS * 2 * MOST), 1)
    spread = jnp.concatenate([jnp.where(lane == target + side * MOST, 1.0, 0.0) for side in range(2)], axis=0)
    both = dot(spread.astype(BF16), ret_ref[...]).astype(BF16)
    out_ref[:, :RET] = both[:ROWS]
    out_ref[:, RET:] = both[ROWS:]


GROUP = 4


GROUPS = HEADS // GROUP


def fetch_weights(group, sources, buffers, sems):
    return [pltpu.make_async_copy(
        src.at[:, pl.ds(pl.multiple_of(group * width, 128), width)], dst.at[group], sems.at[i, group])
        for i, (src, dst, width) in enumerate(zip(sources, buffers, (GROUP * 192, GROUP * 128, GROUP * 128)))]


def rope_tables(extra):
    turned = extra.astype(F32).T
    pos = turned[64:65] * 16.0 + turned[65:66]
    angle = pos * frequencies()
    cos, sin = jnp.cos(angle), jnp.sin(angle)
    return (jnp.concatenate([cos, cos, cos, cos], axis=0).T, jnp.concatenate([-sin, sin, -sin, sin], axis=0).T)


def rotated(rotary, cos, sin):
    lane = iota(rotary.shape, 1) & 63
    swapped = jnp.where(lane < 32, pltpu.roll(rotary, 96, 1), pltpu.roll(rotary, 32, 1))
    return (rotary * cos + swapped * sin).astype(BF16)


def own_kernel(packed_hbm, wq_hbm, wk_hbm, wv_hbm, qn_hbm, qr_hbm, k_hbm, v_hbm,
               qn_ref, qr_ref, k_ref, v_ref, x_ref, wq_ref, wk_ref, wv_ref, cos_ref, sin_ref, x_sem, sems, out_sems):
    def fetch(group):
        return fetch_weights(group, (wq_hbm, wk_hbm, wv_hbm), (wq_ref, wk_ref, wv_ref), sems)

    def send_out(group):
        return [pltpu.make_async_copy(src.at[group], dst.at[group], out_sems.at[i, group]) for i, (src, dst) in enumerate(
            ((qn_ref, qn_hbm), (qr_ref, qr_hbm), (k_ref, k_hbm), (v_ref, v_hbm)))]

    x_copy = pltpu.make_async_copy(packed_hbm, x_ref, x_sem)
    x_copy.start()
    for copy in fetch(0):
        copy.start()
    x_copy.wait()
    for group in range(1, GROUPS):
        for copy in fetch(group):
            copy.start()
    cos_ref[...], sin_ref[...] = rope_tables(x_ref[:, D_Q + D_C:])

    @pl.loop(0, GROUPS)
    def _(group):
        for_queries, for_keys, for_values = fetch(group)
        for_queries.wait()
        queries = dot(x_ref[:, :D_Q], wq_ref[group])
        for pair in range(GROUP // 2):
            even, odd, rotary = split_pair(queries[:, pair * 384:(pair + 1) * 384])
            qn_ref[group, :, pair * 256:pair * 256 + 128] = even.astype(BF16)
            qn_ref[group, :, pair * 256 + 128:pair * 256 + 256] = odd.astype(BF16)
            qr_ref[group, :, pair * 128:(pair + 1) * 128] = rotated(rotary, cos_ref[...], sin_ref[...])
        for_keys.wait()
        for_values.wait()
        latents = x_ref[:, D_Q:D_Q + D_C]
        k_ref[group] = dot(latents, wk_ref[group]).astype(BF16)
        v_ref[group] = dot(latents, wv_ref[group]).astype(BF16)
        for copy in send_out(group):
            copy.start()

    for group in range(GROUPS):
        for copy in send_out(group):
            copy.wait()


def prefill_kernel(right_ref, far_ref, left_ref, own_hbm, wq_hbm, wk_hbm, wv_hbm,
                   own_qn_hbm, own_qr_hbm, own_k_hbm, own_v_hbm, after_ref, out_hbm,
                   own_ref, all_wq_ref, all_wk_ref, all_wv_ref, all_out_ref, chunk_sem, weight_sems, own_sems, out_sems,
                   cos_ref, sin_ref, bias_ref, pair_ref, *sets):
    me = lax.axis_index("head")
    place = [(c - me + 3) & 3 for c in range(4)]
    half = TOKENS // 2
    sets = (sets[:4], sets[4:])
    others = (right_ref, far_ref, left_ref)
    shared_copy = pltpu.make_async_copy(own_hbm.at[:, pl.ds(D_Q + D_C, 128)], own_ref, chunk_sem)

    def fetch(group):
        return fetch_weights(group, (wq_hbm, wk_hbm, wv_hbm), (all_wq_ref, all_wk_ref, all_wv_ref), weight_sems)

    def fetch_own(group, into, parity):
        return [pltpu.make_async_copy(src.at[group], dst.at[3], own_sems.at[i, parity])
                for i, (src, dst) in enumerate(zip((own_qn_hbm, own_qr_hbm, own_k_hbm, own_v_hbm), into))]

    def send_out(group):
        return pltpu.make_async_copy(
            all_out_ref.at[group], out_hbm.at[:, pl.ds(pl.multiple_of(group * GROUP * 128, 128), GROUP * 128)],
            out_sems.at[group])

    def prepare():
        extras = [ref[:, D_Q + D_C:] for ref in others] + [own_ref[...]]
        cos_ref[...], sin_ref[...] = rope_tables(jnp.concatenate(extras[:3], axis=0))
        low_lane = iota((CHUNK, 128), 1) < 64
        for slot, extra in enumerate(extras):
            extra = extra.astype(F32)
            pos = (extra[:, 64:65] * 16.0 + extra[:, 65:66]).astype(jnp.int32)
            chunk = (slot + 1 + me) & 3
            query, key = iota((CHUNK, TOKENS), 0) + chunk * CHUNK, iota((CHUNK, TOKENS), 1)
            bias_ref[chunk] = jnp.where((key <= query) & (key >= query - pos), 0.0, MASKED)
            keep = jnp.where(low_lane, extra, 0.0)
            pair_ref[0, chunk] = keep.astype(BF16)
            pair_ref[1, chunk] = pltpu.roll(keep, 64, 1).astype(BF16)

    def project_steps(into, group):
        qn_ref, qr_ref, k_ref, v_ref = into
        wq_ref, wk_ref, wv_ref = all_wq_ref.at[group], all_wk_ref.at[group], all_wv_ref.at[group]
        rows = 3 * CHUNK
        shape = (3, CHUNK, 128)
        held = []

        def query(first, width):
            x = jnp.concatenate([ref[:, :D_Q] for ref in others], axis=0)
            held.append(dot(x, wq_ref[:, first:first + width]))

        def turn(pair):
            even, odd, rotary = split_pair(jnp.concatenate(held, axis=1)[:, pair * 384:(pair + 1) * 384])
            qn_ref[:3, :, pair * 256:pair * 256 + 128] = even.astype(BF16).reshape(shape)
            qn_ref[:3, :, pair * 256 + 128:pair * 256 + 256] = odd.astype(BF16).reshape(shape)
            qr_ref[:3, :, pair * 128:(pair + 1) * 128] = rotated(rotary, cos_ref[...], sin_ref[...]).reshape(shape)

        def latent(which):
            w_ref, to_ref = ((wk_ref, k_ref), (wv_ref, v_ref))[which - 1]
            x = jnp.concatenate([ref[:, D_Q:D_Q + D_C] for ref in others], axis=0)
            to_ref[:3] = dot(x, w_ref[...]).astype(BF16).reshape(3, CHUNK, GROUP * 128)

        return query, turn, latent

    def attend_steps(source, group):
        qn_ref, qr_ref, k_ref, v_ref = source
        out_ref = all_out_ref.at[group]
        ones = jnp.ones((CHUNK, 128), BF16)
        scores = {}

        def score(head):
            lanes = slice(head * 128, (head + 1) * 128)
            pair = slice(head // 2 * 128, (head // 2 + 1) * 128)
            query = [jnp.concatenate([qn_ref[place[c], :, lanes], qr_ref[place[c], :, pair]], axis=1) for c in range(4)]
            keys = [jnp.concatenate([k_ref[place[c], :, lanes], pair_ref[head % 2, c]], axis=1) for c in range(4)]
            bias = bias_ref[...].reshape(TOKENS, TOKENS)
            early = dot(jnp.concatenate(query, axis=0), jnp.concatenate(keys[:2], axis=0), ((1,), (1,)))
            late = dot(jnp.concatenate(query[2:], axis=0), jnp.concatenate(keys[2:], axis=0), ((1,), (1,)))
            scores[head] = early + bias[:, :half], late + bias[half:, half:]

        def weigh(head):
            lanes = slice(head * 128, (head + 1) * 128)
            early, late = scores[head]
            values = [jnp.concatenate([v_ref[place[c], :, lanes], ones], axis=1) for c in range(4)]
            top = jnp.max(early[:half], axis=1, keepdims=True)
            raised = jnp.exp2((early[:half] - top) * SCALE_LOG2).astype(BF16)
            top_late = jnp.max(jnp.maximum(early[half:], late), axis=1, keepdims=True)
            raised_late = [jnp.exp2((part - top_late) * SCALE_LOG2).astype(BF16) for part in (early[half:], late)]
            total = dot(jnp.concatenate([raised, raised_late[0]], axis=0), jnp.concatenate(values[:2], axis=0))
            total_late = total[half:] + dot(raised_late[1], jnp.concatenate(values[2:], axis=0))
            out_ref[:half, lanes] = (total[:half, :128] / total[:half, 128:]).astype(BF16)
            out_ref[half:, lanes] = (total_late[:, :128] / total_late[:, 128:]).astype(BF16)

        return score, weigh

    def step_copies(copies, act):
        for copy in copies:
            act(copy)

    start, wait = (lambda copy: copy.start()), (lambda copy: copy.wait())
    shared_copy.start()
    step_copies(fetch(0), start)
    shared_copy.wait()
    prepare()
    step_copies(fetch(0), wait)
    step_copies(fetch(1), start)
    step_copies(fetch_own(0, sets[0], 0), start)
    query, turn, latent = project_steps(sets[0], 0)
    query(0, 512)
    query(512, 256)
    turn(0)
    latent(1)
    turn(1)
    latent(2)

    @pl.loop(1, GROUPS)
    def _(step):
        step_copies(fetch(step), wait)

        @pl.when(step < GROUPS - 1)
        def _():
            step_copies(fetch(step + 1), start)

        for parity in range(2):
            @pl.when((step & 1) == parity)
            def _():
                source, into = sets[1 - parity], sets[parity]
                step_copies(fetch_own(step, into, parity), start)
                step_copies(fetch_own(step - 1, source, 1 - parity), wait)
                score, weigh = attend_steps(source, step - 1)
                query, turn, latent = project_steps(into, step)
                query(0, 512)
                score(0)
                score(1)
                weigh(0)
                query(512, 256)
                turn(0)
                score(2)
                weigh(1)
                latent(1)
                turn(1)
                score(3)
                weigh(2)
                latent(2)
                weigh(3)
        send_out(step - 1).start()

    last = GROUPS - 1
    step_copies(fetch_own(last, sets[last % 2], last % 2), wait)
    score, weigh = attend_steps(sets[last % 2], last)
    score(0)
    for head in range(GROUP):
        if head + 1 < GROUP:
            score(head + 1)
        weigh(head)
    send_out(last).start()
    step_copies([send_out(group) for group in range(GROUPS)], wait)


def in_hbm(array):
    return pltpu.with_memory_space_constraint(array, pltpu.HBM)


def whole(shape):
    return pl.BlockSpec(shape, lambda *_: (0,) * len(shape))


def params(mib):
    return pltpu.CompilerParams(vmem_limit_bytes=mib * MIB)


def smem():
    return pl.BlockSpec(memory_space=pltpu.SMEM)


def anywhere():
    return pl.BlockSpec(memory_space=pl.ANY)


def vmem():
    return pl.BlockSpec(memory_space=pltpu.VMEM)


SETS = (GROUP * 128, GROUP * 64, GROUP * 128, GROUP * 128)


WEIGHTS = [pltpu.VMEM((GROUPS, D_Q, GROUP * 192), BF16), pltpu.VMEM((GROUPS, D_C, GROUP * 128), BF16),
           pltpu.VMEM((GROUPS, D_C, GROUP * 128), BF16)]


def project_own(packed, wq, wk, wv):
    return pl.pallas_call(
        own_kernel,
        in_specs=[anywhere()] * 4,
        out_specs=[anywhere()] * 4,
        out_shape=[pltpu.HBM((GROUPS, CHUNK, width), BF16) for width in SETS],
        scratch_shapes=[pltpu.VMEM((GROUPS, CHUNK, width), BF16) for width in SETS]
        + [pltpu.VMEM((CHUNK, PACK), BF16)] + WEIGHTS + [
            pltpu.VMEM((CHUNK, 128), F32),
            pltpu.VMEM((CHUNK, 128), F32),
            pltpu.SemaphoreType.DMA,
            pltpu.SemaphoreType.DMA((3, GROUPS)),
            pltpu.SemaphoreType.DMA((4, GROUPS)),
        ],
        compiler_params=params(60),
        name="own",
    )(in_hbm(packed), wq, wk, wv)


def prefill(right, far, left, packed, wq, wk, wv, own, after):
    return pl.pallas_call(
        prefill_kernel,
        in_specs=[vmem()] * 3 + [anywhere()] * 9,
        out_specs=anywhere(),
        out_shape=jax.ShapeDtypeStruct((TOKENS, HEADS * D_V), BF16),
        scratch_shapes=[pltpu.VMEM((CHUNK, 128), BF16)] + WEIGHTS + [
            pltpu.VMEM((GROUPS, TOKENS, GROUP * 128), BF16),
            pltpu.SemaphoreType.DMA,
            pltpu.SemaphoreType.DMA((3, GROUPS)),
            pltpu.SemaphoreType.DMA((4, 2)),
            pltpu.SemaphoreType.DMA((GROUPS,)),
            pltpu.VMEM((3 * CHUNK, 128), F32),
            pltpu.VMEM((3 * CHUNK, 128), F32),
            pltpu.VMEM((4, CHUNK, TOKENS), F32),
            pltpu.VMEM((2, 4, CHUNK, 128), BF16),
        ] + [pltpu.VMEM((4, CHUNK, width), BF16) for width in SETS] * 2,
        compiler_params=params(36),
        name="prefill",
    )(right, far, left, in_hbm(packed), wq, wk, wv, *own, after)


def on_device(x, latents, rotary_keys, positions, wq, wk, wv, queries, owner, slot, cache, cache_rope, lengths):
    wq, wk, wv, cache, cache_rope = (in_hbm(array) for array in (wq, wk, wv, cache, cache_rope))
    owner_row, slot_row = owner.reshape(1, ROWS), slot.reshape(1, ROWS)
    send, packed, plan = pl.pallas_call(
        stage_kernel,
        in_specs=[anywhere()] * 8,
        out_specs=[anywhere(), anywhere(), vmem()],
        out_shape=[pltpu.HBM((PEERS * 2 * MOST, SEND), BF16), pltpu.HBM((CHUNK, PACK), BF16),
                   jax.ShapeDtypeStruct((1, 2 * SLOTS), jnp.int32)],
        scratch_shapes=[
            pltpu.VMEM((ROWS, HEADS * 192), BF16),
            pltpu.VMEM((1, ROWS), jnp.int32),
            pltpu.VMEM((1, ROWS), jnp.int32),
            pltpu.VMEM((CHUNK, PACK), BF16),
            pltpu.VMEM((64, CHUNK), BF16),
            pltpu.VMEM((1, CHUNK), jnp.int32),
            pltpu.VMEM((1, SLOTS), jnp.int32),
            pltpu.VMEM((PEERS * 2 * MOST, SEND), BF16),
            pltpu.SemaphoreType.DMA((8,)),
            pltpu.SemaphoreType.DMA((2,)),
        ],
        compiler_params=params(60),
        name="stage",
    )(*(in_hbm(array) for array in (
        queries, owner_row, slot_row, x, latents, rotary_keys, positions.reshape(1, CHUNK), lengths.reshape(1, SLOTS))))
    recv = lax.all_to_all(send, "req", 0, 0, tiled=True)
    right = lax.ppermute(packed, "head", [(i, (i + 3) % 4) for i in range(4)])
    left = lax.ppermute(packed, "head", [(i, (i + 1) % 4) for i in range(4)])
    far = lax.ppermute(packed, "head", [(i, (i + 2) % 4) for i in range(4)])
    own = [in_hbm(part) for part in project_own(packed, wq, wk, wv)]

    returned = pl.pallas_call(
        decode_kernel,
        in_specs=[vmem()] + [anywhere()] * 6,
        out_specs=anywhere(),
        out_shape=pltpu.HBM((PEERS * 2 * MOST, RET), BF16),
        scratch_shapes=[
            pltpu.VMEM((D_C, HEADS * D_NOPE + 128), BF16),
            pltpu.VMEM((SLOTS, D_ROPE, CMAX), BF16),
            pltpu.VMEM((D_C, HEADS * D_V + 128), BF16),
            pltpu.VMEM((1, 2 * SLOTS), jnp.int32),
            pltpu.SMEM((1, 2 * SLOTS), jnp.int32),
            pltpu.VMEM((PEERS * 2 * MOST, RET), BF16),
            pltpu.VMEM((SLOTS, CMAX, D_C + 128), BF16),
            pltpu.VMEM((HEADS, SLOTS, D_C), F32),
            pltpu.VMEM((HEADS, SLOTS, 128), F32),
            pltpu.VMEM((HEADS, SLOTS, D_C), F32),
            pltpu.SemaphoreType.DMA((6,)),
            pltpu.SemaphoreType.DMA((SECTIONS, SECTION // TOGETHER)),
            pltpu.SemaphoreType.DMA,
        ],
        compiler_params=params(44),
        name="decode",
    )(recv, wk, cache, cache_rope, wv, in_hbm(plan), own[0])

    prompt_out = prefill(right, far, left, packed, wq, wk, wv, own, in_hbm(returned))
    returned = lax.all_to_all(returned, "req", 0, 0, tiled=True)

    decode_out = pl.pallas_call(
        unplace_kernel,
        out_shape=jax.ShapeDtypeStruct((ROWS, HEADS * D_V), BF16),
        compiler_params=params(16),
        name="unplace",
    )(returned, owner_row)
    return prompt_out, decode_out


def solution(mesh):
    placed = (
        P(("req", "head"), None),
        P(("req", "head"), None),
        P(None, ("req", "head")),
        P(("req", "head")),
        P(None, "head"),
        P(None, "head"),
        P(None, "head"),
        P("req", "head"),
        P("req"),
        P("req"),
        P("req", None, None),
        P("req", None, None),
        P("req"),
    )
    return jax.shard_map(
        on_device,
        mesh=mesh,
        in_specs=placed,
        out_specs=(P("req", "head"), P("req", "head")),
        check_vma=False,
    )
```
